512 devices in a mesh: slab: 32 (over z, x_hi), coil: 16 (over y, x_lo, core).
Axes of the slice: x: 4 (x_hi: 2, x_lo: 2; x = x_hi * 2 + x_lo), y: 4, z: 16, core: 2. Of those that a mesh axis runs over, the one named last changes fastest.
Arguments:
- image_estimate: bfloat16 [2, 2, 8, 512, 512], P(None, None, None, 'slab'), may hold values from -6 to 6
- coil_maps: bfloat16 [2, 32, 8, 512, 512], P(None, 'coil', None, 'slab'), may hold values from -1.5 to 1.5
- measured: bfloat16 [2, 2, 8, 32, 512, 512], P(None, None, None, 'coil', 'slab'), may hold values from -2 to 2
- sampled_blocks: int32 [2, 512, 4], P(None, 'slab'), may hold values 0 or 1
Outputs:
- gradient: float32 [2, 2, 8, 512, 512], P(None, None, None, 'slab')
The draws below stay inside these ranges and needn't reach their ends.
All inputs are finite; a program needn't handle non-finite values. No bound on the sum of `sampled_blocks` on one device may be relied on, other than what follows from the above.
Results may differ from the reference program's by a relative error of at most 0.0034.
Values may be sent and summed in bfloat16 or wider, within the bound.
No kernel may reach another device: no remote copies, remote signals or barrier semaphores. Data moves between devices by JAX's collectives and lax.ppermute only.
A program may use at most 64 MiB of HBM per device.

```python
import math
import jax
import jax.numpy as jnp
from jax import lax

NY = 512
NZ = 512
C = 32
FRAMES = 2
XW = 8
BLOCK = 128
BLOCKS = 4


def plant(values, rng, low, high):
    shape = values.shape
    index_at = [jax.random.randint(jax.random.fold_in(rng, axis), (), 0, shape[axis]) for axis in range(len(shape))]
    values = values.at[tuple(index_at)].set(low)
    longest = shape.index(max(shape))
    index_at[longest] = (index_at[longest] + 1) % shape[longest]
    return values.at[tuple(index_at)].set(high)


def shard_levels(stream_key, shape, pieces, least, top_value):
    loudness, own = 1.0, jax.random.fold_in(stream_key, 6)
    for axis_at, shards_of in pieces:
        steps = jnp.exp(jax.random.uniform(jax.random.fold_in(own, axis_at), (shards_of,), jnp.float32, least / len(pieces), top_value / len(pieces)))
        loudness = loudness * jnp.repeat(steps, shape[axis_at] // shards_of).reshape([-1 if axis == axis_at else 1 for axis in range(len(shape))])
    return loudness


def centred(key, extent, deviation, bound, cuts=(), held_as=jnp.bfloat16):
    result = deviation * jax.random.normal(key, extent, jnp.float32)
    if cuts:
        result = result * shard_levels(key, extent, cuts, -0.22, 0.18)
    return jnp.clip(result, -bound, bound).astype(held_as)


def setup_inputs(seed: int = 0) -> dict:
    seeds = jax.random.split(jax.random.key(seed), 5)
    return {
        "image_estimate": centred(seeds[0], (2, FRAMES, XW, NZ, NY), 1.0, 6.0, ((3, 32),)),
        "coil_maps": centred(seeds[1], (2, C, XW, NZ, NY), 0.25, 1.5, ((1, 16), (3, 32))),
        "measured": centred(seeds[2], (2, FRAMES, XW, C, NY, NZ), 0.3, 2.0, ((3, 16), (4, 32))),
        "sampled_blocks": plant((jax.random.randint(seeds[3], (FRAMES, NY, BLOCKS), 0, 2) < 1).astype(jnp.int32), jax.random.fold_in(seeds[3], 1), 0, 1),
    }


def round_half(value):
    return lax.optimization_barrier(value.astype(jnp.bfloat16)).astype(jnp.float32)

def kernel_tables(length):
    indices = jnp.arange(length, dtype=jnp.int32)
    angles = (indices[:, None] * indices[None, :] % length).astype(jnp.float32) * (2.0 * math.pi / length)
    cosine = round_half(jnp.cos(angles) / math.sqrt(length))
    sinusoid = round_half(jnp.sin(angles) / math.sqrt(length))
    return (cosine, sinusoid)

def last_axis(values, table):
    return jnp.matmul(values, table, precision=lax.Precision.HIGHEST)

def second_axis(values, table):
    return jnp.matmul(table, values, precision=lax.Precision.HIGHEST)

def transform(real_part, imag_part, tables, apply, sign):
    cosine, sinusoid = tables
    cos_re = apply(real_part, cosine)
    cos_im = apply(imag_part, cosine)
    sin_re = apply(real_part, sinusoid)
    sin_im = apply(imag_part, sinusoid)
    return (cos_re + sign * sin_im, cos_im - sign * sin_re)

def reference(image_estimate, coil_maps, measured, sampled_blocks):
    image_re = image_estimate[0].astype(jnp.float32)
    image_im = image_estimate[1].astype(jnp.float32)
    weight = jnp.repeat(sampled_blocks.astype(jnp.float32), BLOCK, axis=2)
    weight = jnp.swapaxes(weight, 1, 2)[:, None]
    maps_all = jnp.moveaxis(coil_maps, 1, 0)
    data_all = jnp.moveaxis(measured, 3, 0)
    tables_y = kernel_tables(NY)
    tables_z = kernel_tables(NZ)

    def one_coil(total, inputs):
        maps_one, data_one = inputs
        map_re = maps_one[0].astype(jnp.float32)
        map_im = maps_one[1].astype(jnp.float32)
        prod_re = round_half(map_re * image_re - map_im * image_im)
        prod_im = round_half(map_re * image_im + map_im * image_re)
        along_re, along_im = transform(prod_re, prod_im, tables_y, last_axis, 1.0)
        along_re = round_half(along_re)
        along_im = round_half(along_im)
        spec_re, spec_im = transform(along_re, along_im, tables_z, second_axis, 1.0)
        target_re = jnp.swapaxes(data_one[0].astype(jnp.float32), -1, -2)
        target_im = jnp.swapaxes(data_one[1].astype(jnp.float32), -1, -2)
        resid_re = round_half(weight * (spec_re - target_re))
        resid_im = round_half(weight * (spec_im - target_im))
        back_re, back_im = transform(resid_re, resid_im, tables_z, second_axis, -1.0)
        back_re = round_half(back_re)
        back_im = round_half(back_im)
        image_back_re, image_back_im = transform(back_re, back_im, tables_y, last_axis, -1.0)
        grad_re = map_re * image_back_re + map_im * image_back_im
        grad_im = map_re * image_back_im - map_im * image_back_re
        return (total + jnp.stack([grad_re, grad_im]).astype(jnp.float32), None)
    start = jnp.zeros(image_estimate.shape, jnp.float32)
    gradient, _ = lax.scan(one_coil, start, (maps_all, data_all))
    return gradient
```

```python
import math

import jax
import jax.numpy as jnp
import ml_dtypes
import numpy as np
from jax import lax
from jax.experimental import pallas as pl
from jax.experimental.pallas import tpu as pltpu
from jax.sharding import PartitionSpec as P

LANES = 128
VMEM_LIMIT = 48 * 1024 * 1024


def dft_tables(length):
    indices = np.arange(length)
    angles = (indices[:, None] * indices[None, :] % length) * (2.0 * math.pi / length)
    cosine = (np.cos(angles) / math.sqrt(length)).astype(ml_dtypes.bfloat16)
    sine = (np.sin(angles) / math.sqrt(length)).astype(ml_dtypes.bfloat16)
    return cosine, sine


def swap_runs(block, run):
    count, rows, lanes = block.shape
    position = lax.broadcasted_iota(jnp.int32, (1, 1, 1, rows, lanes), 4) // run
    step = 1
    while step < count:
        pairs = block.reshape(count // (2 * step), 2, step, rows, lanes)
        low, high = pairs[:, 0:1], pairs[:, 1:2]
        shape = low.shape
        flat = (-1, lanes)
        high_moved = pltpu.roll(high.reshape(flat), step * run, 1).reshape(shape)
        low_moved = pltpu.roll(low.reshape(flat), lanes - step * run, 1).reshape(shape)
        upper = (position & step) != 0
        new_low = jnp.where(upper, high_moved, low)
        new_high = jnp.where(upper, high, low_moved)
        block = jnp.concatenate([new_low, new_high], axis=1).reshape(count, rows, lanes)
        step *= 2
    return block


def forward_y(maps_ref, image_ref, cos_ref, sin_ref, out_ref, lhs):
    coils, readout, z_lo, _ = maps_ref.shape[1:]
    half = readout * coils * z_lo
    for x in range(readout):
        image_re = image_ref[0, 0, x].astype(jnp.float32)
        image_im = image_ref[1, 0, x].astype(jnp.float32)
        for c in range(coils):
            map_re = maps_ref[0, c, x].astype(jnp.float32)
            map_im = maps_ref[1, c, x].astype(jnp.float32)
            row = (x * coils + c) * z_lo
            lhs[row : row + z_lo] = (map_re * image_re - map_im * image_im).astype(jnp.bfloat16)
            row += half
            lhs[row : row + z_lo] = (map_re * image_im + map_im * image_re).astype(jnp.bfloat16)
    by_cos = jnp.dot(lhs[...], cos_ref[...], preferred_element_type=jnp.float32)
    by_sin = jnp.dot(lhs[...], sin_ref[...], preferred_element_type=jnp.float32)
    parts = (by_cos[:half] + by_sin[half:], by_cos[half:] - by_sin[:half])
    group = readout * coils
    run = LANES // group
    for p, part in enumerate(parts):
        for tb in range(part.shape[1] // LANES):
            block = part[:, tb * LANES : (tb + 1) * LANES].reshape(group, z_lo, LANES)
            out_ref[tb * group : (tb + 1) * group, :, p * LANES : (p + 1) * LANES] = swap_runs(
                block, run
            ).astype(jnp.bfloat16)


def z_work(arrived_ref, measured_ref, weight_ref, cos_ref, sin_ref, out_ref, residual):
    blocks = weight_ref.shape[1]
    width = arrived_ref.shape[1] // 2
    depth = arrived_ref.shape[0] // blocks
    by_cos = jnp.dot(cos_ref[...], arrived_ref[...], preferred_element_type=jnp.float32)
    by_sin = jnp.dot(sin_ref[...], arrived_ref[...], preferred_element_type=jnp.float32)
    target_re = measured_ref[0].astype(jnp.float32).T
    target_im = measured_ref[1].astype(jnp.float32).T
    spectrum_re = by_cos[:, :width] + by_sin[:, width:]
    spectrum_im = by_cos[:, width:] - by_sin[:, :width]
    for b in range(blocks):
        rows = slice(b * depth, (b + 1) * depth)
        weight = weight_ref[0, b : b + 1, :]
        residual[rows, :width] = (weight * (spectrum_re[rows] - target_re[rows])).astype(jnp.bfloat16)
        residual[rows, width:] = (weight * (spectrum_im[rows] - target_im[rows])).astype(jnp.bfloat16)
    by_cos = jnp.dot(cos_ref[...], residual[...], preferred_element_type=jnp.float32)
    by_sin = jnp.dot(sin_ref[...], residual[...], preferred_element_type=jnp.float32)
    out_ref[:, :width] = (by_cos[:, :width] - by_sin[:, width:]).astype(jnp.bfloat16)
    out_ref[:, width:] = (by_cos[:, width:] + by_sin[:, :width]).astype(jnp.bfloat16)


def backward_y(returned_ref, maps_ref, cos_ref, sin_ref, out_ref, lhs):
    coils, readout, z_lo, _ = maps_ref.shape[1:]
    half = readout * coils * z_lo
    group = readout * coils
    run = LANES // group
    for p in range(2):
        for tb in range(lhs.shape[1] // LANES):
            block = returned_ref[tb * group : (tb + 1) * group, :, p * LANES : (p + 1) * LANES]
            block = swap_runs(block.astype(jnp.float32), run)
            lhs[p * half : (p + 1) * half, tb * LANES : (tb + 1) * LANES] = block.reshape(
                half, LANES
            ).astype(jnp.bfloat16)
    by_cos = jnp.dot(lhs[...], cos_ref[...], preferred_element_type=jnp.float32)
    by_sin = jnp.dot(lhs[...], sin_ref[...], preferred_element_type=jnp.float32)
    back_re = by_cos[:half] - by_sin[half:]
    back_im = by_cos[half:] + by_sin[:half]
    for x in range(readout):
        sum_re = sum_im = None
        for c in range(coils):
            map_re = maps_ref[0, c, x].astype(jnp.float32)
            map_im = maps_ref[1, c, x].astype(jnp.float32)
            row = (x * coils + c) * z_lo
            re, im = back_re[row : row + z_lo], back_im[row : row + z_lo]
            grad_re = map_re * re + map_im * im
            grad_im = map_re * im - map_im * re
            sum_re = grad_re if sum_re is None else sum_re + grad_re
            sum_im = grad_im if sum_im is None else sum_im + grad_im
        out_ref[x, 0] = sum_re.astype(jnp.bfloat16)
        out_ref[x, 1] = sum_im.astype(jnp.bfloat16)


def coil_sum(terms_ref, out_ref):
    total = jnp.sum(terms_ref[...].astype(jnp.float32), axis=0).astype(jnp.bfloat16)
    out_ref[...] = jnp.broadcast_to(total[None], out_ref.shape)


def call(kernel, name, out_shape, grid, in_specs, out_specs, scratch, flops, bytes_accessed):
    return pl.pallas_call(
        kernel,
        name=name,
        out_shape=out_shape,
        grid=grid,
        in_specs=in_specs,
        out_specs=out_specs,
        scratch_shapes=scratch,
        compiler_params=pltpu.CompilerParams(
            dimension_semantics=("arbitrary",), vmem_limit_bytes=VMEM_LIMIT
        ),
        cost_estimate=pl.CostEstimate(
            flops=flops, bytes_accessed=bytes_accessed, transcendentals=0
        ),
    )


def shards(image_estimate, coil_maps, measured, sampled_blocks, cosine, sine):
    slabs = lax.axis_size("slab")
    groups = lax.axis_size("coil")
    _, frames, readout, z_lo, len_y = image_estimate.shape
    coils = coil_maps.shape[1]
    ky_lo, len_z = measured.shape[4:]
    block_count = sampled_blocks.shape[2]
    group = LANES // ky_lo
    part = group // coils
    parts = readout // part
    steps = frames * parts
    lanes = steps * 2 * LANES
    half = group * z_lo

    maps_spec = pl.BlockSpec((2, coils, part, z_lo, len_y), lambda i: (0, 0, i % parts, 0, 0))
    image_spec = pl.BlockSpec((2, 1, part, z_lo, len_y), lambda i: (0, i // parts, i % parts, 0, 0))
    table_spec = pl.BlockSpec((len_y, len_y), lambda i: (0, 0))
    turned_spec = pl.BlockSpec((slabs, z_lo, 2 * LANES), lambda i: (0, 0, i))
    columns_spec = pl.BlockSpec((len_z, 2 * LANES), lambda i: (0, i))
    table_bytes = 4 * len_y * len_y

    outgoing = call(
        forward_y,
        "forward_y",
        jax.ShapeDtypeStruct((slabs, z_lo, lanes), jnp.bfloat16),
        (steps,),
        [maps_spec, image_spec, table_spec, table_spec],
        turned_spec,
        [pltpu.VMEM((2 * half, len_y), jnp.bfloat16)],
        8 * steps * half * len_y * len_y,
        8 * steps * half * len_y + table_bytes,
    )(coil_maps, image_estimate, cosine, sine)
    arrived = lax.all_to_all(outgoing, "slab", split_axis=0, concat_axis=0, tiled=True)

    weight = jnp.swapaxes(sampled_blocks.astype(jnp.float32), 1, 2)
    weight = jnp.tile(weight, (1, 1, group))
    back_z = call(
        z_work,
        "z_work",
        jax.ShapeDtypeStruct((len_z, lanes), jnp.bfloat16),
        (steps,),
        [
            columns_spec,
            pl.BlockSpec((2, LANES, len_z), lambda i: (0, i, 0)),
            pl.BlockSpec((1, block_count, LANES), lambda i: (i // parts, 0, 0)),
            table_spec,
            table_spec,
        ],
        columns_spec,
        [pltpu.VMEM((len_z, 2 * LANES), jnp.bfloat16)],
        16 * steps * half * len_z * len_z,
        12 * steps * half * len_z + table_bytes,
    )(
        arrived.reshape(len_z, lanes),
        measured.reshape(2, steps * LANES, len_z),
        weight,
        cosine,
        sine,
    )
    returned = lax.all_to_all(
        back_z.reshape(slabs, z_lo, lanes), "slab", split_axis=0, concat_axis=0, tiled=True
    )

    partial_sum = call(
        backward_y,
        "backward_y",
        jax.ShapeDtypeStruct((frames * readout, 2, z_lo, len_y), jnp.bfloat16),
        (steps,),
        [turned_spec, maps_spec, table_spec, table_spec],
        pl.BlockSpec((part, 2, z_lo, len_y), lambda i: (i, 0, 0, 0)),
        [pltpu.VMEM((2 * half, len_y), jnp.bfloat16)],
        8 * steps * half * len_y * len_y,
        8 * steps * half * len_y + table_bytes,
    )(returned, coil_maps, cosine, sine)

    pieces = frames * readout // groups
    rows = pieces * 2 * z_lo
    terms = lax.all_to_all(partial_sum, "coil", split_axis=0, concat_axis=0, tiled=True)
    sum_spec = pl.BlockSpec((groups, rows, len_y), lambda i: (0, 0, 0))
    total = call(
        coil_sum,
        "coil_sum",
        jax.ShapeDtypeStruct((groups, rows, len_y), jnp.bfloat16),
        (1,),
        [sum_spec],
        sum_spec,
        [],
        groups * rows * len_y,
        4 * groups * rows * len_y,
    )(terms.reshape(groups, rows, len_y))
    whole = lax.all_to_all(total, "coil", split_axis=0, concat_axis=0, tiled=True)
    whole = whole.reshape(frames, readout, 2, z_lo, len_y)
    return jnp.moveaxis(whole, 2, 0).astype(jnp.float32)


def solution(mesh):
    body = jax.shard_map(
        shards,
        mesh=mesh,
        in_specs=(
            P(None, None, None, "slab", None),
            P(None, "coil", None, "slab", None),
            P(None, None, None, "coil", "slab", None),
            P(None, "slab", None),
            P(None, None),
            P(None, None),
        ),
        out_specs=P(None, None, None, "slab", None),
        check_vma=False,
    )

    def run(image_estimate, coil_maps, measured, sampled_blocks):
        cosine, sine = dft_tables(image_estimate.shape[4])
        return body(
            image_estimate, coil_maps, measured, sampled_blocks, jnp.asarray(cosine), jnp.asarray(sine)
        )

    return run
```

```python
import math

import jax
import jax.numpy as jnp
import ml_dtypes
import numpy as np
from jax import lax
from jax.experimental import pallas as pl
from jax.experimental.pallas import tpu as pltpu
from jax.sharding import PartitionSpec as P

LANES = 128
VMEM_LIMIT = 48 * 1024 * 1024


def dft_tables(length):
    indices = np.arange(length)
    angles = (indices[:, None] * indices[None, :] % length) * (2.0 * math.pi / length)
    cosine = (np.cos(angles) / math.sqrt(length)).astype(ml_dtypes.bfloat16)
    sine = (np.sin(angles) / math.sqrt(length)).astype(ml_dtypes.bfloat16)
    return cosine, sine


def swap_runs(block, run):
    count, rows, lanes = block.shape
    position = lax.broadcasted_iota(jnp.int32, (1, 1, 1, rows, lanes), 4) // run
    step = 1
    while step < count:
        pairs = block.reshape(count // (2 * step), 2, step, rows, lanes)
        low, high = pairs[:, 0:1], pairs[:, 1:2]
        shape = low.shape
        flat = (-1, lanes)
        high_moved = pltpu.roll(high.reshape(flat), step * run, 1).reshape(shape)
        low_moved = pltpu.roll(low.reshape(flat), lanes - step * run, 1).reshape(shape)
        upper = (position & step) != 0
        new_low = jnp.where(upper, high_moved, low)
        new_high = jnp.where(upper, high, low_moved)
        block = jnp.concatenate([new_low, new_high], axis=1).reshape(count, rows, lanes)
        step *= 2
    return block


def forward_y(maps_ref, image_ref, cos_ref, sin_ref, out_ref, lhs):
    coils, readout, z_lo, _ = maps_ref.shape[1:]
    frames = image_ref.shape[1]
    group = readout * frames * coils
    half = group * z_lo
    for x in range(readout):
        for f in range(frames):
            image_re = image_ref[0, f, x].astype(jnp.float32)
            image_im = image_ref[1, f, x].astype(jnp.float32)
            for c in range(coils):
                map_re = maps_ref[0, c, x].astype(jnp.float32)
                map_im = maps_ref[1, c, x].astype(jnp.float32)
                row = ((x * frames + f) * coils + c) * z_lo
                lhs[row : row + z_lo] = (map_re * image_re - map_im * image_im).astype(jnp.bfloat16)
                row += half
                lhs[row : row + z_lo] = (map_re * image_im + map_im * image_re).astype(jnp.bfloat16)
    by_cos = jnp.dot(lhs[...], cos_ref[...], preferred_element_type=jnp.float32)
    by_sin = jnp.dot(lhs[...], sin_ref[...], preferred_element_type=jnp.float32)
    parts = (by_cos[:half] + by_sin[half:], by_cos[half:] - by_sin[:half])
    run = LANES // group
    for p, part in enumerate(parts):
        for tb in range(part.shape[1] // LANES):
            block = part[:, tb * LANES : (tb + 1) * LANES].reshape(group, z_lo, LANES)
            out_ref[tb * group : (tb + 1) * group, :, p * LANES : (p + 1) * LANES] = swap_runs(
                block, run
            ).astype(jnp.bfloat16)


def z_work(arrived_ref, measured_ref, weight_ref, cos_ref, sin_ref, out_ref, residual):
    blocks = weight_ref.shape[0]
    width = arrived_ref.shape[1] // 2
    depth = arrived_ref.shape[0] // blocks
    _, frames, readout, coils, ky_lo, len_z = measured_ref.shape
    by_cos = jnp.dot(cos_ref[...], arrived_ref[...], preferred_element_type=jnp.float32)
    by_sin = jnp.dot(sin_ref[...], arrived_ref[...], preferred_element_type=jnp.float32)
    target = []
    for p in range(2):
        rows = [
            measured_ref[p, f, x].astype(jnp.float32).reshape(coils * ky_lo, len_z)
            for x in range(readout)
            for f in range(frames)
        ]
        target.append(jnp.concatenate(rows, axis=0).T)
    spectrum_re = by_cos[:, :width] + by_sin[:, width:]
    spectrum_im = by_cos[:, width:] - by_sin[:, :width]
    for b in range(blocks):
        rows = slice(b * depth, (b + 1) * depth)
        weight = weight_ref[b : b + 1, :]
        residual[rows, :width] = (weight * (spectrum_re[rows] - target[0][rows])).astype(jnp.bfloat16)
        residual[rows, width:] = (weight * (spectrum_im[rows] - target[1][rows])).astype(jnp.bfloat16)
    by_cos = jnp.dot(cos_ref[...], residual[...], preferred_element_type=jnp.float32)
    by_sin = jnp.dot(sin_ref[...], residual[...], preferred_element_type=jnp.float32)
    back_re = by_cos[:, :width] - by_sin[:, width:]
    back_im = by_cos[:, width:] + by_sin[:, :width]
    run = width // readout
    lower = lax.broadcasted_iota(jnp.int32, back_re.shape, 1) < run
    slabs, z_lo = out_ref.shape[0], out_ref.shape[2]
    for x, part in enumerate(
        (
            jnp.where(lower, back_re, pltpu.roll(back_im, run, 1)),
            jnp.where(lower, pltpu.roll(back_re, run, 1), back_im),
        )
    ):
        out_ref[:, x] = part.reshape(slabs, z_lo, width).astype(jnp.bfloat16)


def backward_y(place_ref, returned_ref, maps_ref, cos_ref, sin_ref, out_ref, lhs, total):
    step = pl.program_id(0)
    chip, core = place_ref[0], place_ref[1]
    chips, rows = returned_ref.shape[1:3]
    cores, _, coils, z_part, _ = maps_ref.shape[1:]
    frames = total.shape[1]
    group = 2 * frames * coils
    run = LANES // group
    half = lhs.shape[0] // 2

    @pl.when(step == 0)
    def _():
        total[...] = jnp.zeros_like(total)

    for q in range(chips):
        for tb in range(lhs.shape[1] // LANES):
            block = returned_ref[tb * group : (tb + 1) * group, q].astype(jnp.float32)
            block = swap_runs(block, run).astype(jnp.bfloat16)
            for p in range(2):
                for f in range(frames):
                    for c in range(coils):
                        row = p * half + ((f * chips + q) * coils + c) * rows
                        lhs[row : row + rows, tb * LANES : (tb + 1) * LANES] = block[
                            (p * frames + f) * coils + c
                        ]
    by_cos = jnp.dot(lhs[...], cos_ref[...], preferred_element_type=jnp.float32)
    by_sin = jnp.dot(lhs[...], sin_ref[...], preferred_element_type=jnp.float32)
    back_re = by_cos[:half] - by_sin[half:]
    back_im = by_cos[half:] + by_sin[:half]
    sums = [[total[0, f], total[1, f]] for f in range(frames)]
    for q in range(chips):
        source = (step * chips + q) ^ chip
        for k in range(cores):
            for c in range(coils):
                map_re = maps_ref[source, k ^ core, 0, c].astype(jnp.float32)
                map_im = maps_ref[source, k ^ core, 1, c].astype(jnp.float32)
                for f in range(frames):
                    row = ((f * chips + q) * coils + c) * rows + k * z_part
                    re, im = back_re[row : row + z_part], back_im[row : row + z_part]
                    sums[f][0] = sums[f][0] + (map_re * re + map_im * im)
                    sums[f][1] = sums[f][1] + (map_re * im - map_im * re)
    for f in range(frames):
        total[0, f] = sums[f][0]
        total[1, f] = sums[f][1]

    @pl.when(step == pl.num_programs(0) - 1)
    def _():
        whole = jnp.concatenate([total[p, f] for p in range(2) for f in range(frames)], axis=0)
        out_ref[...] = jnp.broadcast_to(whole.astype(jnp.bfloat16)[None], out_ref.shape)


def call(kernel, name, out_shape, grid_spec, flops, bytes_accessed):
    return pl.pallas_call(
        kernel,
        name=name,
        out_shape=out_shape,
        grid_spec=grid_spec,
        compiler_params=pltpu.CompilerParams(
            dimension_semantics=("arbitrary",), vmem_limit_bytes=VMEM_LIMIT
        ),
        cost_estimate=pl.CostEstimate(
            flops=flops, bytes_accessed=bytes_accessed, transcendentals=0
        ),
    )


def maps_by_readout(coil_maps, place):
    cores = 2
    chips = lax.axis_size("coil") // cores
    chip, core = place[0], place[1]
    _, coils, readout, z_lo, len_y = coil_maps.shape
    halves = coil_maps.reshape(2, coils, readout, cores, z_lo // cores, len_y)
    own = lax.dynamic_index_in_dim(halves, core, 3, keepdims=False)
    other = lax.dynamic_index_in_dim(halves, 1 - core, 3, keepdims=False)
    devices = range(chips * cores)
    got = lax.ppermute(other, "coil", [(i, i ^ 1) for i in devices])
    both = jnp.stack([own, got])
    pieces = []
    for k in range(chips):
        piece = lax.dynamic_index_in_dim(both, chip ^ k, 3, keepdims=False)
        if k:
            piece = lax.ppermute(piece, "coil", [(i, i ^ (cores * k)) for i in devices])
        pieces.append(piece)
    return jnp.stack(pieces)


def shards(image_estimate, coil_maps, measured, sampled_blocks, cosine, sine):
    slabs = lax.axis_size("slab")
    groups = lax.axis_size("coil")
    _, frames, readout, z_lo, len_y = image_estimate.shape
    coils = coil_maps.shape[1]
    ky_lo, len_z = measured.shape[4:]
    block_count = sampled_blocks.shape[2]
    group = LANES // ky_lo
    part = group // (coils * frames)
    steps = readout // part
    lanes = steps * 2 * LANES
    half = group * z_lo
    cores = 2
    chips = groups // cores
    z_part = z_lo // cores
    me = lax.axis_index("coil")
    place = jnp.stack([me // cores, me % cores]).astype(jnp.int32)

    maps_spec = pl.BlockSpec((2, coils, part, z_lo, len_y), lambda i: (0, 0, i, 0, 0))
    image_spec = pl.BlockSpec((2, frames, part, z_lo, len_y), lambda i: (0, 0, i, 0, 0))
    table_spec = pl.BlockSpec((len_y, len_y), lambda i: (0, 0))
    table_bytes = 4 * len_y * len_y

    outgoing = call(
        forward_y,
        "forward_y",
        jax.ShapeDtypeStruct((slabs, z_lo, lanes), jnp.bfloat16),
        pl.GridSpec(
            grid=(steps,),
            in_specs=[maps_spec, image_spec, table_spec, table_spec],
            out_specs=pl.BlockSpec((slabs, z_lo, 2 * LANES), lambda i: (0, 0, i)),
            scratch_shapes=[pltpu.VMEM((2 * half, len_y), jnp.bfloat16)],
        ),
        8 * steps * half * len_y * len_y,
        8 * steps * half * len_y + table_bytes,
    )(coil_maps, image_estimate, cosine, sine)
    outgoing, late_maps = lax.optimization_barrier((outgoing, coil_maps))
    arrived = lax.all_to_all(outgoing, "slab", split_axis=0, concat_axis=0, tiled=True)
    own_maps = maps_by_readout(late_maps, place)

    weight = jnp.transpose(sampled_blocks.astype(jnp.float32), (2, 0, 1))[:, None, :, None, :]
    weight = jnp.broadcast_to(weight, (block_count, part, frames, coils, ky_lo))
    back_z = call(
        z_work,
        "z_work",
        jax.ShapeDtypeStruct((slabs, readout, z_lo, LANES), jnp.bfloat16),
        pl.GridSpec(
            grid=(steps,),
            in_specs=[
                pl.BlockSpec((len_z, 2 * LANES), lambda i: (0, i)),
                pl.BlockSpec(
                    (2, frames, part, coils, ky_lo, len_z), lambda i: (0, 0, i, 0, 0, 0)
                ),
                pl.BlockSpec((block_count, LANES), lambda i: (0, 0)),
                table_spec,
                table_spec,
            ],
            out_specs=pl.BlockSpec((slabs, part, z_lo, LANES), lambda i: (0, i, 0, 0)),
            scratch_shapes=[pltpu.VMEM((len_z, 2 * LANES), jnp.bfloat16)],
        ),
        16 * steps * half * len_z * len_z,
        12 * steps * half * len_z + table_bytes,
    )(
        arrived.reshape(len_z, lanes),
        measured,
        weight.reshape(block_count, LANES),
        cosine,
        sine,
    )
    returned = lax.all_to_all(
        back_z.reshape(slabs * groups, z_part, LANES),
        ("slab", "coil"),
        split_axis=0,
        concat_axis=0,
        tiled=True,
    )

    pair = 2
    rows = 2 * frames * z_part
    total = call(
        backward_y,
        "backward_y",
        jax.ShapeDtypeStruct((groups, rows, len_y), jnp.bfloat16),
        pltpu.PrefetchScalarGridSpec(
            num_scalar_prefetch=1,
            grid=(chips // pair,),
            in_specs=[
                pl.BlockSpec((slabs, pair, z_lo, LANES), lambda i, s: (0, i, 0, 0)),
                pl.BlockSpec(
                    (chips, cores, 2, coils, z_part, len_y), lambda i, s: (0, 0, 0, 0, 0, 0)
                ),
                pl.BlockSpec((len_y, len_y), lambda i, s: (0, 0)),
                pl.BlockSpec((len_y, len_y), lambda i, s: (0, 0)),
            ],
            out_specs=pl.BlockSpec((groups, rows, len_y), lambda i, s: (0, 0, 0)),
            scratch_shapes=[
                pltpu.VMEM((2 * frames * pair * coils * z_lo, len_y), jnp.bfloat16),
                pltpu.VMEM((2, frames, z_part, len_y), jnp.float32),
            ],
        ),
        8 * steps * half * len_y * len_y,
        8 * steps * half * len_y + table_bytes,
    )(place, returned.reshape(slabs, chips, z_lo, LANES), own_maps, cosine, sine)

    whole = lax.all_to_all(total, "coil", split_axis=0, concat_axis=0, tiled=True)
    whole = whole.reshape(readout, cores, 2, frames, z_part, len_y)
    whole = jnp.transpose(whole, (2, 3, 0, 1, 4, 5)).astype(jnp.float32)
    return whole.reshape(2, frames, readout, z_lo, len_y)


def solution(mesh):
    body = jax.shard_map(
        shards,
        mesh=mesh,
        in_specs=(
            P(None, None, None, "slab", None),
            P(None, "coil", None, "slab", None),
            P(None, None, None, "coil", "slab", None),
            P(None, "slab", None),
            P(None, None),
            P(None, None),
        ),
        out_specs=P(None, None, None, "slab", None),
        check_vma=False,
    )

    def run(image_estimate, coil_maps, measured, sampled_blocks):
        cosine, sine = dft_tables(image_estimate.shape[4])
        return body(
            image_estimate, coil_maps, measured, sampled_blocks, jnp.asarray(cosine), jnp.asarray(sine)
        )

    return run
```

```python
import math

import jax
import jax.numpy as jnp
import ml_dtypes
import numpy as np
from jax import lax
from jax.experimental import pallas as pl
from jax.experimental.pallas import tpu as pltpu
from jax.sharding import PartitionSpec as P

LANES = 128
VMEM_SOME = 40 * 1024 * 1024
VMEM_ALL = 62 * 1024 * 1024


def dft_tables(length):
    indices = np.arange(length)
    angles = (indices[:, None] * indices[None, :] % length) * (2.0 * math.pi / length)
    cosine = (np.cos(angles) / math.sqrt(length)).astype(ml_dtypes.bfloat16)
    sine = (np.sin(angles) / math.sqrt(length)).astype(ml_dtypes.bfloat16)
    return cosine, sine


def swap_runs(blocks, run):
    count = len(blocks)
    rows, lanes = blocks[0].shape
    position = lax.broadcasted_iota(jnp.int32, (rows, lanes), 1) // run
    moved = [pltpu.roll(b, i * run, 1) if i else b for i, b in enumerate(blocks)]
    moved = [moved[-k % count] for k in range(count)]
    step = 1
    while step < count:
        chosen = (position & step) != 0
        moved = [jnp.where(chosen, moved[(k - step) % count], moved[k]) for k in range(count)]
        step *= 2
    return [pltpu.roll(b, lanes - j * run, 1) if j else b for j, b in enumerate(moved)]


def forward_y(maps_ref, image_ref, cos_ref, sin_ref, out_ref, lhs):
    _, coils, readout, z_lo, len_y = maps_ref.shape
    frames = image_ref.shape[1]
    steps = lhs.shape[0]
    part = readout // steps
    group = part * frames * coils
    half = group * z_lo
    run = LANES // group
    for i in range(steps):
        for x in range(part):
            for f in range(frames):
                image_re = image_ref[0, f, i * part + x].astype(jnp.float32)
                image_im = image_ref[1, f, i * part + x].astype(jnp.float32)
                for c in range(coils):
                    map_re = maps_ref[0, c, i * part + x].astype(jnp.float32)
                    map_im = maps_ref[1, c, i * part + x].astype(jnp.float32)
                    row = ((x * frames + f) * coils + c) * z_lo
                    coil_re = map_re * image_re - map_im * image_im
                    coil_im = map_re * image_im + map_im * image_re
                    lhs[i, row : row + z_lo] = coil_re.astype(jnp.bfloat16)
                    lhs[i, row + half : row + half + z_lo] = coil_im.astype(jnp.bfloat16)
        by_cos = jnp.dot(lhs[i], cos_ref[...], preferred_element_type=jnp.float32)
        by_sin = jnp.dot(lhs[i], sin_ref[...], preferred_element_type=jnp.float32)
        for p, along in enumerate((by_cos[:half] + by_sin[half:], by_cos[half:] - by_sin[:half])):
            lane = (2 * i + p) * LANES
            for t in range(len_y // LANES):
                block = along[:, t * LANES : (t + 1) * LANES]
                block = [block[u * z_lo : (u + 1) * z_lo] for u in range(group)]
                for u, rows in enumerate(swap_runs(block, run)):
                    out_ref[t * group + u, :, lane : lane + LANES] = rows.astype(jnp.bfloat16)


def z_work(arrived_ref, measured_ref, weight_ref, cos_ref, sin_ref, out_ref, residual):
    _, frames, readout, coils, ky_lo, len_z = measured_ref.shape
    blocks = weight_ref.shape[0]
    width = weight_ref.shape[1]
    depth = len_z // blocks
    steps = arrived_ref.shape[1] // (2 * width)
    part = readout // steps
    slabs, _, z_lo, _ = out_ref.shape
    for i in range(steps):
        mid, end = (2 * i + 1) * width, (2 * i + 2) * width
        arrived = arrived_ref[:, mid - width : end]
        by_cos = jnp.dot(cos_ref[...], arrived, preferred_element_type=jnp.float32)
        by_sin = jnp.dot(sin_ref[...], arrived, preferred_element_type=jnp.float32)
        target = []
        for p in range(2):
            lines = [
                measured_ref[p, f, i * part + x].reshape(coils * ky_lo, len_z)
                for x in range(part)
                for f in range(frames)
            ]
            target.append(jnp.concatenate(lines, axis=0).T.astype(jnp.float32))
        spectrum_re = by_cos[:, :width] + by_sin[:, width:]
        spectrum_im = by_cos[:, width:] - by_sin[:, :width]
        for b in range(blocks):
            rows = slice(b * depth, (b + 1) * depth)
            weight = weight_ref[b : b + 1, :]
            resid_re = weight * (spectrum_re[rows] - target[0][rows])
            resid_im = weight * (spectrum_im[rows] - target[1][rows])
            residual[rows, mid - width : mid] = resid_re.astype(jnp.bfloat16)
            residual[rows, mid:end] = resid_im.astype(jnp.bfloat16)
    run = width // part
    lower = lax.broadcasted_iota(jnp.int32, (len_z, width), 1) < run
    for i in range(steps):
        rows = residual[:, 2 * i * width : (2 * i + 2) * width]
        by_cos = jnp.dot(cos_ref[...], rows, preferred_element_type=jnp.float32)
        by_sin = jnp.dot(sin_ref[...], rows, preferred_element_type=jnp.float32)
        back_re = by_cos[:, :width] - by_sin[:, width:]
        back_im = by_cos[:, width:] + by_sin[:, :width]
        sent = (
            jnp.where(lower, back_re, pltpu.roll(back_im, run, 1)),
            jnp.where(lower, pltpu.roll(back_re, run, 1), back_im),
        )
        for x in range(part):
            out_ref[:, i * part + x] = sent[x].reshape(slabs, z_lo, width).astype(jnp.bfloat16)


def backward_y(place_ref, returned_ref, maps_ref, cos_ref, sin_ref, out_ref, lhs):
    chip, core = place_ref[0], place_ref[1]
    _, chips, rows, _ = returned_ref.shape
    _, cores, _, coils, z_part, len_y = maps_ref.shape
    steps, height, _ = lhs.shape
    pair = chips // steps
    half = height // 2
    frames = half // (pair * coils * rows)
    group = 2 * frames * coils
    run = LANES // group
    zero = jnp.zeros((z_part, len_y), jnp.float32)
    sums = [[zero, zero] for _ in range(frames)]
    for i in range(steps):
        for q in range(pair):
            for t in range(len_y // LANES):
                block = returned_ref[t * group : (t + 1) * group, i * pair + q].astype(jnp.float32)
                block = swap_runs([block[u] for u in range(group)], run)
                for p in range(2):
                    for f in range(frames):
                        for c in range(coils):
                            row = p * half + ((f * pair + q) * coils + c) * rows
                            lhs[i, row : row + rows, t * LANES : (t + 1) * LANES] = block[
                                (p * frames + f) * coils + c
                            ].astype(jnp.bfloat16)
        by_cos = jnp.dot(lhs[i], cos_ref[...], preferred_element_type=jnp.float32)
        by_sin = jnp.dot(lhs[i], sin_ref[...], preferred_element_type=jnp.float32)
        back_re = by_cos[:half] - by_sin[half:]
        back_im = by_cos[half:] + by_sin[:half]
        for q in range(pair):
            source = (i * pair + q) ^ chip
            for k in range(cores):
                for c in range(coils):
                    map_re = maps_ref[source, k ^ core, 0, c].astype(jnp.float32)
                    map_im = maps_ref[source, k ^ core, 1, c].astype(jnp.float32)
                    for f in range(frames):
                        row = ((f * pair + q) * coils + c) * rows + k * z_part
                        re, im = back_re[row : row + z_part], back_im[row : row + z_part]
                        sums[f][0] = sums[f][0] + (map_re * re + map_im * im)
                        sums[f][1] = sums[f][1] + (map_re * im - map_im * re)
    whole = jnp.concatenate([sums[f][p] for p in range(2) for f in range(frames)], axis=0)
    out_ref[...] = jnp.broadcast_to(whole.astype(jnp.bfloat16)[None], out_ref.shape)


def call(kernel, name, out_shape, in_spaces, out_space, scratch, flops, bytes_accessed, vmem):
    return pl.pallas_call(
        kernel,
        name=name,
        out_shape=out_shape,
        in_specs=[pl.BlockSpec(memory_space=space) for space in in_spaces],
        out_specs=pl.BlockSpec(memory_space=out_space),
        scratch_shapes=scratch,
        compiler_params=pltpu.CompilerParams(vmem_limit_bytes=vmem),
        cost_estimate=pl.CostEstimate(
            flops=flops, bytes_accessed=bytes_accessed, transcendentals=0
        ),
    )


def maps_by_readout(coil_maps, place):
    cores = 2
    chips = lax.axis_size("coil") // cores
    chip, core = place[0], place[1]
    _, coils, readout, z_lo, len_y = coil_maps.shape
    halves = coil_maps.reshape(2, coils, readout, cores, z_lo // cores, len_y)
    own = lax.dynamic_index_in_dim(halves, core, 3, keepdims=False)
    other = lax.dynamic_index_in_dim(halves, 1 - core, 3, keepdims=False)
    devices = range(chips * cores)
    got = lax.ppermute(other, "coil", [(i, i ^ 1) for i in devices])
    both = jnp.stack([own, got])
    pieces = []
    for k in range(chips):
        piece = lax.dynamic_index_in_dim(both, chip ^ k, 3, keepdims=False)
        if k:
            piece = lax.ppermute(piece, "coil", [(i, i ^ (cores * k)) for i in devices])
        pieces.append(piece)
    return jnp.stack(pieces)


def send_forward(coil_maps, image_estimate, cosine, sine, slabs):
    _, frames, readout, z_lo, len_y = image_estimate.shape
    coils = coil_maps.shape[1]
    group = LANES // (len_y // slabs)
    part = group // (coils * frames)
    steps = readout // part
    half = group * z_lo
    return call(
        forward_y,
        "forward_y",
        jax.ShapeDtypeStruct((slabs, z_lo, steps * 2 * LANES), jnp.bfloat16),
        [pltpu.VMEM] * 4,
        pltpu.VMEM,
        [pltpu.VMEM((steps, 2 * half, len_y), jnp.bfloat16)],
        8 * steps * half * len_y * len_y,
        8 * steps * half * len_y + 4 * len_y * len_y,
        VMEM_ALL,
    )(coil_maps, image_estimate, cosine, sine)


def send_back(arrived, measured, sampled_blocks, cosine, sine):
    slabs, z_lo, lanes = arrived.shape
    _, frames, readout, coils, ky_lo, len_z = measured.shape
    block_count = sampled_blocks.shape[2]
    steps = lanes // (2 * LANES)
    part = readout // steps
    weight = jnp.transpose(sampled_blocks.astype(jnp.float32), (2, 0, 1))[:, None, :, None, :]
    weight = jnp.broadcast_to(weight, (block_count, part, frames, coils, ky_lo))
    return call(
        z_work,
        "z_work",
        jax.ShapeDtypeStruct((slabs, readout, z_lo, LANES), jnp.bfloat16),
        [pltpu.VMEM] * 5,
        pltpu.VMEM,
        [pltpu.VMEM((len_z, lanes), jnp.bfloat16)],
        8 * lanes * len_z * len_z,
        6 * lanes * len_z + 4 * len_z * len_z,
        VMEM_SOME,
    )(
        arrived.reshape(len_z, lanes),
        measured,
        weight.reshape(block_count, LANES),
        cosine,
        sine,
    )


def combine(returned, own_maps, place, cosine, sine):
    slabs, chips, z_lo, _ = returned.shape
    _, cores, _, coils, z_part, len_y = own_maps.shape
    frames = LANES // (len_y // slabs * 2 * coils)
    pair = 2
    steps = chips // pair
    height = 2 * frames * pair * coils * z_lo
    return call(
        backward_y,
        "backward_y",
        jax.ShapeDtypeStruct((chips * cores, 2 * frames * z_part, len_y), jnp.bfloat16),
        [pltpu.SMEM] + [pltpu.VMEM] * 4,
        pltpu.VMEM,
        [pltpu.VMEM((steps, height, len_y), jnp.bfloat16)],
        4 * steps * height * len_y * len_y,
        4 * steps * height * len_y + 4 * len_y * len_y,
        VMEM_SOME,
    )(place, returned, own_maps, cosine, sine)


def shards(image_estimate, coil_maps, measured, sampled_blocks, cosine, sine):
    slabs = lax.axis_size("slab")
    groups = lax.axis_size("coil")
    _, frames, readout, z_lo, len_y = image_estimate.shape
    cores = 2
    z_part = z_lo // cores
    me = lax.axis_index("coil")
    place = jnp.stack([me // cores, me % cores]).astype(jnp.int32)

    outgoing = send_forward(coil_maps, image_estimate, cosine, sine, slabs)
    outgoing, late_maps = lax.optimization_barrier((outgoing, coil_maps))
    arrived = lax.all_to_all(outgoing, "slab", split_axis=0, concat_axis=0, tiled=True)
    own_maps = maps_by_readout(late_maps, place)
    back_z = send_back(arrived, measured, sampled_blocks, cosine, sine)
    returned = lax.all_to_all(
        back_z.reshape(slabs * groups, z_part, LANES),
        ("slab", "coil"),
        split_axis=0,
        concat_axis=0,
        tiled=True,
    )
    total = combine(
        returned.reshape(slabs, groups // cores, z_lo, LANES), own_maps, place, cosine, sine
    )
    whole = lax.all_to_all(total, "coil", split_axis=0, concat_axis=0, tiled=True)
    whole = whole.reshape(readout, cores, 2, frames, z_part, len_y)
    whole = jnp.transpose(whole, (2, 3, 0, 1, 4, 5)).astype(jnp.float32)
    return whole.reshape(2, frames, readout, z_lo, len_y)


def solution(mesh):
    body = jax.shard_map(
        shards,
        mesh=mesh,
        in_specs=(
            P(None, None, None, "slab", None),
            P(None, "coil", None, "slab", None),
            P(None, None, None, "coil", "slab", None),
            P(None, "slab", None),
            P(None, None),
            P(None, None),
        ),
        out_specs=P(None, None, None, "slab", None),
        check_vma=False,
    )

    def run(image_estimate, coil_maps, measured, sampled_blocks):
        cosine, sine = dft_tables(image_estimate.shape[4])
        return body(
            image_estimate, coil_maps, measured, sampled_blocks, jnp.asarray(cosine), jnp.asarray(sine)
        )

    return run
```

```python
import math

import jax
import jax.numpy as jnp
import ml_dtypes
import numpy as np
from jax import lax
from jax.experimental import pallas as pl
from jax.experimental.pallas import tpu as pltpu
from jax.sharding import PartitionSpec as P

LANES = 128
VMEM_SOME = 40 * 1024 * 1024
VMEM_ALL = 62 * 1024 * 1024


def dft_tables(length, run):
    indices = np.arange(length)
    angles = (indices[:, None] * indices[None, :] % length) * (2.0 * math.pi / length)
    cosine = (np.cos(angles) / math.sqrt(length)).astype(ml_dtypes.bfloat16)
    sine = (np.sin(angles) / math.sqrt(length)).astype(ml_dtypes.bfloat16)
    middle = length // 2
    turned = indices.reshape(-1, run).copy()
    turned[middle // run :] = turned[middle // run :, ::-1]
    turned = turned.reshape(-1)
    half_cos = cosine[:, :middle]
    half_sin = sine[:, :middle].copy()
    half_sin[:, 0] = cosine[:, middle]
    tables = (
        np.concatenate([half_cos, half_sin]),
        np.concatenate([half_cos.T, half_sin.T]),
        np.concatenate([cosine[turned], sine[turned]]),
    )
    return tuple(np.ascontiguousarray(table) for table in tables)


def mirror(values, axis):
    middle = values.shape[axis] // 2
    first = lax.slice_in_dim(values, 0, middle + 1, axis=axis)
    last = lax.slice_in_dim(values, middle + 1, 2 * middle, axis=axis)
    return lax.concatenate([first, lax.rev(last, (axis,))], axis)


def split_ends(by_cos, by_sin, axis):
    edge = (8, LANES)[axis]
    cos_edge = lax.slice_in_dim(by_cos, 0, edge, axis=axis)
    sin_edge = lax.slice_in_dim(by_sin, 0, edge, axis=axis)
    first = lax.broadcasted_iota(jnp.int32, cos_edge.shape, axis) == 0
    joined = []
    for edge_values, values in (
        (jnp.where(first, sin_edge, cos_edge), by_cos),
        (jnp.where(first, jnp.zeros_like(sin_edge), sin_edge), by_sin),
    ):
        rest = lax.slice_in_dim(values, edge, values.shape[axis], axis=axis)
        joined.append(jnp.concatenate([edge_values, rest], axis=axis))
    return joined


def swap_runs(blocks, run):
    count = len(blocks)
    rows, lanes = blocks[0].shape
    position = lax.broadcasted_iota(jnp.int32, (rows, lanes), 1) // run
    moved = [pltpu.roll(b, i * run, 1) if i else b for i, b in enumerate(blocks)]
    moved = [moved[-k % count] for k in range(count)]
    step = 1
    while step < count:
        chosen = (position & step) != 0
        moved = [jnp.where(chosen, moved[(k - step) % count], moved[k]) for k in range(count)]
        step *= 2
    return [pltpu.roll(b, lanes - j * run, 1) if j else b for j, b in enumerate(moved)]


def forward_y(maps_ref, image_ref, table_ref, out_ref, lhs):
    _, coils, readout, z_lo, len_y = maps_ref.shape
    frames = image_ref.shape[1]
    steps = lhs.shape[0]
    part = readout // steps
    group = part * frames * coils
    half = group * z_lo
    run = LANES // group
    for i in range(steps):
        for x in range(part):
            for f in range(frames):
                image_re = image_ref[0, f, i * part + x].astype(jnp.float32)
                image_im = image_ref[1, f, i * part + x].astype(jnp.float32)
                for c in range(coils):
                    map_re = maps_ref[0, c, i * part + x].astype(jnp.float32)
                    map_im = maps_ref[1, c, i * part + x].astype(jnp.float32)
                    row = ((x * frames + f) * coils + c) * z_lo
                    coil_re = map_re * image_re - map_im * image_im
                    coil_im = map_re * image_im + map_im * image_re
                    lhs[i, row : row + z_lo] = coil_re.astype(jnp.bfloat16)
                    lhs[i, row + half : row + half + z_lo] = coil_im.astype(jnp.bfloat16)
        by_cos = jnp.dot(lhs[i], table_ref[:len_y], preferred_element_type=jnp.float32)
        by_sin = jnp.dot(lhs[i], table_ref[len_y:], preferred_element_type=jnp.float32)
        middle = by_cos.shape[1]
        other_cos, by_sin = split_ends(by_cos, by_sin, 1)
        lower = (by_cos[:half] + by_sin[half:], by_cos[half:] - by_sin[:half])
        upper = (other_cos[:half] - by_sin[half:], other_cos[half:] + by_sin[:half])
        final = lax.broadcasted_iota(jnp.int32, (half, LANES), 1) == LANES - 1
        for p in range(2):
            lane = (2 * i + p) * LANES
            blocks = [lower[p][:, t * LANES : (t + 1) * LANES] for t in range(middle // LANES)]
            moved = [
                pltpu.roll(upper[p][:, t * LANES : (t + 1) * LANES], LANES - 1, 1)
                for t in range(middle // LANES)
            ]
            for t in range(len(moved)):
                blocks.append(jnp.where(final, moved[(t + 1) % len(moved)], moved[t]))
            for t, block in enumerate(blocks):
                block = [block[u * z_lo : (u + 1) * z_lo] for u in range(group)]
                for u, rows in enumerate(swap_runs(block, run)):
                    slab = t * group + u
                    if t >= len(moved):
                        slab = out_ref.shape[0] - 1 - (t - len(moved)) * group - u
                    out_ref[slab, :, lane : lane + LANES] = rows.astype(jnp.bfloat16)


def z_work(
    arrived_ref,
    measured_ref,
    weight_ref,
    columns_ref,
    rows_ref,
    out_ref,
    table,
    residual,
    out,
    leave,
):
    _, frames, readout, coils, ky_lo, len_z = measured_ref.shape
    width = weight_ref.shape[1]
    middle = len_z // 2
    steps = arrived_ref.shape[1] // (2 * width)
    part = readout // steps
    slabs, _, z_lo, _ = out_ref.shape
    for i in range(steps):
        start, mid, end = 2 * i * width, (2 * i + 1) * width, (2 * i + 2) * width
        arrived = arrived_ref[:, start:end]
        by_cos = jnp.dot(rows_ref[:middle], arrived, preferred_element_type=jnp.float32)
        by_sin = jnp.dot(rows_ref[middle:], arrived, preferred_element_type=jnp.float32)
        other_cos, by_sin = split_ends(by_cos, by_sin, 0)
        target = []
        for p in range(2):
            lines = [
                measured_ref[p, f, i * part + x].reshape(coils * ky_lo, len_z)
                for x in range(part)
                for f in range(frames)
            ]
            target.append(jnp.concatenate(lines, axis=0).T.astype(jnp.float32))
        for rows, spectrum_re, spectrum_im in (
            (
                slice(0, middle),
                by_cos[:, :width] + by_sin[:, width:],
                by_cos[:, width:] - by_sin[:, :width],
            ),
            (
                slice(middle, len_z),
                other_cos[:, :width] - by_sin[:, width:],
                other_cos[:, width:] + by_sin[:, :width],
            ),
        ):
            weight = weight_ref[rows]
            residual[rows, start:mid] = (weight * (spectrum_re - target[0][rows])).astype(jnp.bfloat16)
            residual[rows, mid:end] = (weight * (spectrum_im - target[1][rows])).astype(jnp.bfloat16)
    run = width // part
    lower = lax.broadcasted_iota(jnp.int32, (len_z, width), 1) < run
    half_cos, half_sin = columns_ref[:len_z], columns_ref[len_z:]
    other_cos, half_sin = split_ends(half_cos, half_sin, 1)
    table[:len_z, :middle] = half_cos
    table[:len_z, middle:] = other_cos
    table[len_z:, :middle] = half_sin
    table[len_z:, middle:] = -half_sin
    copies = []
    for i in range(steps):
        rows = residual[:, 2 * i * width : (2 * i + 2) * width]
        by_cos = jnp.dot(table[:len_z], rows, preferred_element_type=jnp.float32)
        by_sin = jnp.dot(table[len_z:], rows, preferred_element_type=jnp.float32)
        back_re = by_cos[:, :width] - by_sin[:, width:]
        back_im = by_cos[:, width:] + by_sin[:, :width]
        sent = (
            jnp.where(lower, back_re, pltpu.roll(back_im, run, 1)),
            jnp.where(lower, pltpu.roll(back_re, run, 1), back_im),
        )
        for x in range(part):
            out[:, i * part + x] = sent[x].reshape(slabs, z_lo, width).astype(jnp.bfloat16)
        here = pl.ds(i * part, part)
        copies.append(pltpu.make_async_copy(out.at[:, here], out_ref.at[:, here], leave.at[i]))
        copies[-1].start()
    for copy in copies:
        copy.wait()


def backward_y(place_ref, returned_ref, maps_ref, table_ref, out_ref, lhs):
    chip, core = place_ref[0], place_ref[1]
    _, chips, rows, _ = returned_ref.shape
    _, cores, _, coils, z_part, len_y = maps_ref.shape
    steps, height, _ = lhs.shape
    pair = chips // steps
    half = height // 2
    frames = half // (pair * coils * rows)
    group = 2 * frames * coils
    run = LANES // group
    zero = jnp.zeros((z_part, len_y), jnp.float32)
    sums = [[zero, zero] for _ in range(frames)]
    for i in range(steps):
        for q in range(pair):
            for t in range(len_y // LANES):
                block = returned_ref[t * group : (t + 1) * group, i * pair + q].astype(jnp.float32)
                block = swap_runs([block[u] for u in range(group)], run)
                for p in range(2):
                    for f in range(frames):
                        for c in range(coils):
                            row = p * half + ((f * pair + q) * coils + c) * rows
                            lhs[i, row : row + rows, t * LANES : (t + 1) * LANES] = block[
                                (p * frames + f) * coils + c
                            ].astype(jnp.bfloat16)
        by_cos = jnp.dot(lhs[i], table_ref[:len_y], preferred_element_type=jnp.float32)
        by_sin = jnp.dot(lhs[i], table_ref[len_y:], preferred_element_type=jnp.float32)
        back_re = by_cos[:half] - by_sin[half:]
        back_im = by_cos[half:] + by_sin[:half]
        for q in range(pair):
            source = (i * pair + q) ^ chip
            for k in range(cores):
                for c in range(coils):
                    map_re = maps_ref[source, k ^ core, 0, c].astype(jnp.float32)
                    map_im = maps_ref[source, k ^ core, 1, c].astype(jnp.float32)
                    for f in range(frames):
                        row = ((f * pair + q) * coils + c) * rows + k * z_part
                        re, im = back_re[row : row + z_part], back_im[row : row + z_part]
                        sums[f][0] = sums[f][0] + (map_re * re + map_im * im)
                        sums[f][1] = sums[f][1] + (map_re * im - map_im * re)
    whole = jnp.concatenate([sums[f][p] for p in range(2) for f in range(frames)], axis=0)
    out_ref[...] = jnp.broadcast_to(whole.astype(jnp.bfloat16)[None], out_ref.shape)


def call(kernel, name, out_shape, in_spaces, out_space, scratch, flops, bytes_accessed, vmem):
    return pl.pallas_call(
        kernel,
        name=name,
        out_shape=out_shape,
        in_specs=[pl.BlockSpec(memory_space=space) for space in in_spaces],
        out_specs=pl.BlockSpec(memory_space=out_space),
        scratch_shapes=scratch,
        compiler_params=pltpu.CompilerParams(vmem_limit_bytes=vmem),
        cost_estimate=pl.CostEstimate(
            flops=flops, bytes_accessed=bytes_accessed, transcendentals=0
        ),
    )


def maps_by_readout(coil_maps, place):
    cores = 2
    chips = lax.axis_size("coil") // cores
    chip, core = place[0], place[1]
    _, coils, readout, z_lo, len_y = coil_maps.shape
    halves = coil_maps.reshape(2, coils, readout, cores, z_lo // cores, len_y)
    own = lax.dynamic_index_in_dim(halves, core, 3, keepdims=False)
    other = lax.dynamic_index_in_dim(halves, 1 - core, 3, keepdims=False)
    devices = range(chips * cores)
    got = lax.ppermute(other, "coil", [(i, i ^ 1) for i in devices])
    both = jnp.stack([own, got])
    pieces = []
    for k in range(chips):
        piece = lax.dynamic_index_in_dim(both, chip ^ k, 3, keepdims=False)
        if k:
            piece = lax.ppermute(piece, "coil", [(i, i ^ (cores * k)) for i in devices])
        pieces.append(piece)
    return jnp.stack(pieces)


def send_forward(coil_maps, image_estimate, table, slabs):
    _, frames, readout, z_lo, len_y = image_estimate.shape
    coils = coil_maps.shape[1]
    group = LANES // (len_y // slabs)
    part = group // (coils * frames)
    steps = readout // part
    half = group * z_lo
    return call(
        forward_y,
        "forward_y",
        jax.ShapeDtypeStruct((slabs, z_lo, steps * 2 * LANES), jnp.bfloat16),
        [pltpu.VMEM] * 3,
        pltpu.VMEM,
        [pltpu.VMEM((steps, 2 * half, len_y), jnp.bfloat16)],
        4 * steps * half * len_y * len_y,
        8 * steps * half * len_y + 2 * len_y * len_y,
        VMEM_ALL,
    )(coil_maps, image_estimate, table)


def send_back(arrived, measured, sampled_blocks, columns, rows):
    slabs, z_lo, lanes = arrived.shape
    _, frames, readout, coils, ky_lo, len_z = measured.shape
    block_count = sampled_blocks.shape[2]
    steps = lanes // (2 * LANES)
    part = readout // steps
    weight = jnp.transpose(sampled_blocks.astype(jnp.float32), (2, 0, 1))[:, None, :, None, :]
    weight = jnp.broadcast_to(weight, (block_count, part, frames, coils, ky_lo))
    weight = jnp.repeat(weight.reshape(block_count, LANES), len_z // block_count, axis=0)
    return call(
        z_work,
        "z_work",
        jax.ShapeDtypeStruct((slabs, readout, z_lo, LANES), jnp.bfloat16),
        [pltpu.VMEM] * 5,
        pl.ANY,
        [
            pltpu.VMEM((2 * len_z, len_z), jnp.bfloat16),
            pltpu.VMEM((len_z, lanes), jnp.bfloat16),
            pltpu.VMEM((slabs, readout, z_lo, LANES), jnp.bfloat16),
            pltpu.SemaphoreType.DMA((steps,)),
        ],
        6 * lanes * len_z * len_z,
        6 * lanes * len_z + 4 * len_z * len_z,
        VMEM_SOME,
    )(arrived.reshape(len_z, lanes), measured, mirror(weight, 0), columns, rows)


def combine(returned, own_maps, place, table):
    slabs, chips, z_lo, _ = returned.shape
    _, cores, _, coils, z_part, len_y = own_maps.shape
    frames = LANES // (len_y // slabs * 2 * coils)
    pair = 2
    steps = chips // pair
    height = 2 * frames * pair * coils * z_lo
    return call(
        backward_y,
        "backward_y",
        jax.ShapeDtypeStruct((chips * cores, 2 * frames * z_part, len_y), jnp.bfloat16),
        [pltpu.SMEM] + [pltpu.VMEM] * 3,
        pltpu.VMEM,
        [pltpu.VMEM((steps, height, len_y), jnp.bfloat16)],
        4 * steps * height * len_y * len_y,
        4 * steps * height * len_y + 4 * len_y * len_y,
        VMEM_SOME,
    )(place, returned, own_maps, table)


def shards(image_estimate, coil_maps, measured, sampled_blocks, *tables):
    slabs = lax.axis_size("slab")
    groups = lax.axis_size("coil")
    _, frames, readout, z_lo, len_y = image_estimate.shape
    cores = 2
    z_part = z_lo // cores
    me = lax.axis_index("coil")
    place = jnp.stack([me // cores, me % cores]).astype(jnp.int32)

    outgoing = send_forward(coil_maps, image_estimate, tables[0], slabs)
    outgoing, coil_maps, measured, sampled_blocks = lax.optimization_barrier(
        (outgoing, coil_maps, measured, sampled_blocks)
    )
    arrived = lax.all_to_all(outgoing, "slab", split_axis=0, concat_axis=0, tiled=True)
    own_maps = maps_by_readout(coil_maps, place)
    upper = lax.axis_index("slab") >= slabs // 2
    measured = jnp.where(upper, lax.rev(measured, (4,)), measured)
    sampled_blocks = jnp.where(upper, lax.rev(sampled_blocks, (1,)), sampled_blocks)
    back_z = send_back(arrived, mirror(measured, 5), sampled_blocks, *tables[:2])
    returned = lax.all_to_all(
        back_z.reshape(slabs * groups, z_part, LANES),
        ("slab", "coil"),
        split_axis=0,
        concat_axis=0,
        tiled=True,
    )
    total = combine(
        returned.reshape(slabs, groups // cores, z_lo, LANES), own_maps, place, tables[2]
    )
    whole = lax.all_to_all(total, "coil", split_axis=0, concat_axis=0, tiled=True)
    whole = whole.reshape(readout, cores, 2, frames, z_part, len_y)
    whole = jnp.transpose(whole, (2, 3, 0, 1, 4, 5)).astype(jnp.float32)
    return whole.reshape(2, frames, readout, z_lo, len_y)


def solution(mesh):
    body = jax.shard_map(
        shards,
        mesh=mesh,
        in_specs=(
            P(None, None, None, "slab", None),
            P(None, "coil", None, "slab", None),
            P(None, None, None, "coil", "slab", None),
            P(None, "slab", None),
            *[P(None, None)] * 3,
        ),
        out_specs=P(None, None, None, "slab", None),
        check_vma=False,
    )

    def run(image_estimate, coil_maps, measured, sampled_blocks):
        slabs, len_y = mesh.shape["slab"], image_estimate.shape[4]
        tables = [jnp.asarray(table) for table in dft_tables(len_y, len_y // slabs)]
        return body(image_estimate, coil_maps, measured, sampled_blocks, *tables)

    return run
```

```python
import math

import jax
import jax.numpy as jnp
import ml_dtypes
import numpy as np
from jax import lax
from jax.experimental import pallas as pl
from jax.experimental.pallas import tpu as pltpu
from jax.sharding import PartitionSpec as P

LANES = 128
VMEM_SOME = 40 * 1024 * 1024
VMEM_ALL = 62 * 1024 * 1024


def dft_tables(length, run):
    indices = np.arange(length)
    angles = (indices[:, None] * indices[None, :] % length) * (2.0 * math.pi / length)
    cosine = (np.cos(angles) / math.sqrt(length)).astype(ml_dtypes.bfloat16)
    sine = (np.sin(angles) / math.sqrt(length)).astype(ml_dtypes.bfloat16)
    middle = length // 2
    turned = indices.reshape(-1, run).copy()
    turned[middle // run :] = turned[middle // run :, ::-1]
    turned = turned.reshape(-1)
    half_cos = cosine[:, :middle]
    half_sin = sine[:, :middle].copy()
    half_sin[:, 0] = cosine[:, middle]
    tables = (
        np.concatenate([half_cos, half_sin]),
        np.concatenate([half_cos.T, half_sin.T]),
        np.concatenate([cosine[turned], sine[turned]]),
    )
    return tuple(np.ascontiguousarray(table) for table in tables)


def mirror(values, axis):
    middle = values.shape[axis] // 2
    first = lax.slice_in_dim(values, 0, middle + 1, axis=axis)
    last = lax.slice_in_dim(values, middle + 1, 2 * middle, axis=axis)
    return lax.concatenate([first, lax.rev(last, (axis,))], axis)


def split_ends(by_cos, by_sin, axis):
    edge = (8, LANES)[axis]
    cos_edge = lax.slice_in_dim(by_cos, 0, edge, axis=axis)
    sin_edge = lax.slice_in_dim(by_sin, 0, edge, axis=axis)
    first = lax.broadcasted_iota(jnp.int32, cos_edge.shape, axis) == 0
    joined = []
    for edge_values, values in (
        (jnp.where(first, sin_edge, cos_edge), by_cos),
        (jnp.where(first, jnp.zeros_like(sin_edge), sin_edge), by_sin),
    ):
        rest = lax.slice_in_dim(values, edge, values.shape[axis], axis=axis)
        joined.append(jnp.concatenate([edge_values, rest], axis=axis))
    return joined


def swap_runs(blocks, run):
    count = len(blocks)
    rows, lanes = blocks[0].shape
    position = lax.broadcasted_iota(jnp.int32, (rows, lanes), 1) // run
    moved = [pltpu.roll(b, i * run, 1) if i else b for i, b in enumerate(blocks)]
    moved = [moved[-k % count] for k in range(count)]
    step = 1
    while step < count:
        chosen = (position & step) != 0
        moved = [jnp.where(chosen, moved[(k - step) % count], moved[k]) for k in range(count)]
        step *= 2
    return [pltpu.roll(b, lanes - j * run, 1) if j else b for j, b in enumerate(moved)]


def forward_y(
    maps_ref, image_ref, table_ref, out_ref, maps, image, table, lhs, out, arrive, leave
):
    _, coils, readout, z_lo, len_y = maps_ref.shape
    frames = image_ref.shape[1]
    steps = lhs.shape[0]
    part = readout // steps
    group = part * frames * coils
    half = group * z_lo
    run = LANES // group
    inputs = [
        pltpu.make_async_copy(source, held, arrive.at[k])
        for k, (source, held) in enumerate(((maps_ref, maps), (image_ref, image), (table_ref, table)))
    ]
    for copy in inputs:
        copy.start()
    inputs[0].wait()
    inputs[1].wait()
    for i in range(steps):
        for x in range(part):
            for f in range(frames):
                image_re = image[0, f, i * part + x].astype(jnp.float32)
                image_im = image[1, f, i * part + x].astype(jnp.float32)
                for c in range(coils):
                    map_re = maps[0, c, i * part + x].astype(jnp.float32)
                    map_im = maps[1, c, i * part + x].astype(jnp.float32)
                    row = ((x * frames + f) * coils + c) * z_lo
                    coil_re = map_re * image_re - map_im * image_im
                    coil_im = map_re * image_im + map_im * image_re
                    lhs[i, row : row + z_lo] = coil_re.astype(jnp.bfloat16)
                    lhs[i, row + half : row + half + z_lo] = coil_im.astype(jnp.bfloat16)
    inputs[2].wait()
    results = []
    for i in range(steps):
        by_cos = jnp.dot(lhs[i], table[:len_y], preferred_element_type=jnp.float32)
        by_sin = jnp.dot(lhs[i], table[len_y:], preferred_element_type=jnp.float32)
        middle = by_cos.shape[1]
        other_cos, by_sin = split_ends(by_cos, by_sin, 1)
        lower = (by_cos[:half] + by_sin[half:], by_cos[half:] - by_sin[:half])
        upper = (other_cos[:half] - by_sin[half:], other_cos[half:] + by_sin[:half])
        final = lax.broadcasted_iota(jnp.int32, (half, LANES), 1) == LANES - 1
        for p in range(2):
            lane = p * LANES
            blocks = [lower[p][:, t * LANES : (t + 1) * LANES] for t in range(middle // LANES)]
            moved = [
                pltpu.roll(upper[p][:, t * LANES : (t + 1) * LANES], LANES - 1, 1)
                for t in range(middle // LANES)
            ]
            for t in range(len(moved)):
                blocks.append(jnp.where(final, moved[(t + 1) % len(moved)], moved[t]))
            for t, block in enumerate(blocks):
                block = [block[u * z_lo : (u + 1) * z_lo] for u in range(group)]
                for u, rows in enumerate(swap_runs(block, run)):
                    slab = t * group + u
                    if t >= len(moved):
                        slab = out.shape[1] - 1 - (t - len(moved)) * group - u
                    out[i, slab, :, lane : lane + LANES] = rows.astype(jnp.bfloat16)
        lanes = pl.ds(2 * i * LANES, 2 * LANES)
        results.append(pltpu.make_async_copy(out.at[i], out_ref.at[:, :, lanes], leave.at[i]))
        results[-1].start()
    for copy in results:
        copy.wait()


def z_work(
    arrived_ref,
    measured_ref,
    weight_ref,
    columns_ref,
    rows_ref,
    out_ref,
    table,
    residual,
    out,
    leave,
):
    _, frames, readout, coils, ky_lo, len_z = measured_ref.shape
    width = weight_ref.shape[1]
    middle = len_z // 2
    steps = arrived_ref.shape[1] // (2 * width)
    part = readout // steps
    slabs, _, z_lo, _ = out_ref.shape
    for i in range(steps):
        start, mid, end = 2 * i * width, (2 * i + 1) * width, (2 * i + 2) * width
        arrived = arrived_ref[:, start:end]
        by_cos = jnp.dot(rows_ref[:middle], arrived, preferred_element_type=jnp.float32)
        by_sin = jnp.dot(rows_ref[middle:], arrived, preferred_element_type=jnp.float32)
        other_cos, by_sin = split_ends(by_cos, by_sin, 0)
        target = []
        for p in range(2):
            lines = [
                measured_ref[p, f, i * part + x].reshape(coils * ky_lo, len_z)
                for x in range(part)
                for f in range(frames)
            ]
            target.append(jnp.concatenate(lines, axis=0).T.astype(jnp.float32))
        for rows, spectrum_re, spectrum_im in (
            (
                slice(0, middle),
                by_cos[:, :width] + by_sin[:, width:],
                by_cos[:, width:] - by_sin[:, :width],
            ),
            (
                slice(middle, len_z),
                other_cos[:, :width] - by_sin[:, width:],
                other_cos[:, width:] + by_sin[:, :width],
            ),
        ):
            weight = weight_ref[rows]
            residual[rows, start:mid] = (weight * (spectrum_re - target[0][rows])).astype(jnp.bfloat16)
            residual[rows, mid:end] = (weight * (spectrum_im - target[1][rows])).astype(jnp.bfloat16)
    run = width // part
    lower = lax.broadcasted_iota(jnp.int32, (len_z, width), 1) < run
    half_cos, half_sin = columns_ref[:len_z], columns_ref[len_z:]
    other_cos, half_sin = split_ends(half_cos, half_sin, 1)
    table[:len_z, :middle] = half_cos
    table[:len_z, middle:] = other_cos
    table[len_z:, :middle] = half_sin
    table[len_z:, middle:] = -half_sin
    copies = []
    for i in range(steps):
        rows = residual[:, 2 * i * width : (2 * i + 2) * width]
        by_cos = jnp.dot(table[:len_z], rows, preferred_element_type=jnp.float32)
        by_sin = jnp.dot(table[len_z:], rows, preferred_element_type=jnp.float32)
        back_re = by_cos[:, :width] - by_sin[:, width:]
        back_im = by_cos[:, width:] + by_sin[:, :width]
        sent = (
            jnp.where(lower, back_re, pltpu.roll(back_im, run, 1)),
            jnp.where(lower, pltpu.roll(back_re, run, 1), back_im),
        )
        for x in range(part):
            out[:, i * part + x] = sent[x].reshape(slabs, z_lo, width).astype(jnp.bfloat16)
        here = pl.ds(i * part, part)
        copies.append(pltpu.make_async_copy(out.at[:, here], out_ref.at[:, here], leave.at[i]))
        copies[-1].start()
    for copy in copies:
        copy.wait()


def backward_y(place_ref, returned_ref, maps_ref, table_ref, out_ref, lhs):
    chip, core = place_ref[0], place_ref[1]
    _, chips, rows, _ = returned_ref.shape
    _, cores, _, coils, z_part, len_y = maps_ref.shape
    steps, height, _ = lhs.shape
    pair = chips // steps
    half = height // 2
    frames = half // (pair * coils * rows)
    group = 2 * frames * coils
    run = LANES // group
    zero = jnp.zeros((z_part, len_y), jnp.float32)
    sums = [[zero, zero] for _ in range(frames)]
    for i in range(steps):
        for q in range(pair):
            for t in range(len_y // LANES):
                block = returned_ref[t * group : (t + 1) * group, i * pair + q].astype(jnp.float32)
                block = swap_runs([block[u] for u in range(group)], run)
                for p in range(2):
                    for f in range(frames):
                        for c in range(coils):
                            row = p * half + ((f * pair + q) * coils + c) * rows
                            lhs[i, row : row + rows, t * LANES : (t + 1) * LANES] = block[
                                (p * frames + f) * coils + c
                            ].astype(jnp.bfloat16)
        by_cos = jnp.dot(lhs[i], table_ref[:len_y], preferred_element_type=jnp.float32)
        by_sin = jnp.dot(lhs[i], table_ref[len_y:], preferred_element_type=jnp.float32)
        back_re = by_cos[:half] - by_sin[half:]
        back_im = by_cos[half:] + by_sin[:half]
        for q in range(pair):
            source = (i * pair + q) ^ chip
            for k in range(cores):
                for c in range(coils):
                    map_re = maps_ref[source, k ^ core, 0, c].astype(jnp.float32)
                    map_im = maps_ref[source, k ^ core, 1, c].astype(jnp.float32)
                    for f in range(frames):
                        row = ((f * pair + q) * coils + c) * rows + k * z_part
                        re, im = back_re[row : row + z_part], back_im[row : row + z_part]
                        sums[f][0] = sums[f][0] + (map_re * re + map_im * im)
                        sums[f][1] = sums[f][1] + (map_re * im - map_im * re)
    whole = jnp.concatenate([sums[f][p] for p in range(2) for f in range(frames)], axis=0)
    out_ref[...] = jnp.broadcast_to(whole.astype(jnp.bfloat16)[None], out_ref.shape)


def call(kernel, name, out_shape, in_spaces, out_space, scratch, flops, bytes_accessed, vmem):
    return pl.pallas_call(
        kernel,
        name=name,
        out_shape=out_shape,
        in_specs=[pl.BlockSpec(memory_space=space) for space in in_spaces],
        out_specs=pl.BlockSpec(memory_space=out_space),
        scratch_shapes=scratch,
        compiler_params=pltpu.CompilerParams(vmem_limit_bytes=vmem),
        cost_estimate=pl.CostEstimate(
            flops=flops, bytes_accessed=bytes_accessed, transcendentals=0
        ),
    )


def maps_by_readout(coil_maps, place):
    cores = 2
    chips = lax.axis_size("coil") // cores
    chip, core = place[0], place[1]
    _, coils, readout, z_lo, len_y = coil_maps.shape
    halves = coil_maps.reshape(2, coils, readout, cores, z_lo // cores, len_y)
    own = lax.dynamic_index_in_dim(halves, core, 3, keepdims=False)
    other = lax.dynamic_index_in_dim(halves, 1 - core, 3, keepdims=False)
    devices = range(chips * cores)
    got = lax.ppermute(other, "coil", [(i, i ^ 1) for i in devices])
    both = jnp.stack([own, got])
    pieces = []
    for k in range(chips):
        piece = lax.dynamic_index_in_dim(both, chip ^ k, 3, keepdims=False)
        if k:
            piece = lax.ppermute(piece, "coil", [(i, i ^ (cores * k)) for i in devices])
        pieces.append(piece)
    return jnp.stack(pieces)


def send_forward(coil_maps, image_estimate, table, slabs):
    _, frames, readout, z_lo, len_y = image_estimate.shape
    coils = coil_maps.shape[1]
    group = LANES // (len_y // slabs)
    part = group // (coils * frames)
    steps = readout // part
    half = group * z_lo
    return call(
        forward_y,
        "forward_y",
        jax.ShapeDtypeStruct((slabs, z_lo, steps * 2 * LANES), jnp.bfloat16),
        [pl.ANY] * 3,
        pl.ANY,
        [
            pltpu.VMEM(coil_maps.shape, jnp.bfloat16),
            pltpu.VMEM(image_estimate.shape, jnp.bfloat16),
            pltpu.VMEM(table.shape, jnp.bfloat16),
            pltpu.VMEM((steps, 2 * half, len_y), jnp.bfloat16),
            pltpu.VMEM((steps, slabs, z_lo, 2 * LANES), jnp.bfloat16),
            pltpu.SemaphoreType.DMA((3,)),
            pltpu.SemaphoreType.DMA((steps,)),
        ],
        4 * steps * half * len_y * len_y,
        8 * steps * half * len_y + 2 * len_y * len_y,
        VMEM_ALL,
    )(coil_maps, image_estimate, table)


def send_back(arrived, measured, sampled_blocks, columns, rows):
    slabs, z_lo, lanes = arrived.shape
    _, frames, readout, coils, ky_lo, len_z = measured.shape
    block_count = sampled_blocks.shape[2]
    steps = lanes // (2 * LANES)
    part = readout // steps
    weight = jnp.transpose(sampled_blocks.astype(jnp.float32), (2, 0, 1))[:, None, :, None, :]
    weight = jnp.broadcast_to(weight, (block_count, part, frames, coils, ky_lo))
    weight = jnp.repeat(weight.reshape(block_count, LANES), len_z // block_count, axis=0)
    return call(
        z_work,
        "z_work",
        jax.ShapeDtypeStruct((slabs, readout, z_lo, LANES), jnp.bfloat16),
        [pltpu.VMEM] * 5,
        pl.ANY,
        [
            pltpu.VMEM((2 * len_z, len_z), jnp.bfloat16),
            pltpu.VMEM((len_z, lanes), jnp.bfloat16),
            pltpu.VMEM((slabs, readout, z_lo, LANES), jnp.bfloat16),
            pltpu.SemaphoreType.DMA((steps,)),
        ],
        6 * lanes * len_z * len_z,
        6 * lanes * len_z + 4 * len_z * len_z,
        VMEM_SOME,
    )(arrived.reshape(len_z, lanes), measured, mirror(weight, 0), columns, rows)


def combine(returned, own_maps, place, table):
    slabs, chips, z_lo, _ = returned.shape
    _, cores, _, coils, z_part, len_y = own_maps.shape
    frames = LANES // (len_y // slabs * 2 * coils)
    pair = 2
    steps = chips // pair
    height = 2 * frames * pair * coils * z_lo
    return call(
        backward_y,
        "backward_y",
        jax.ShapeDtypeStruct((chips * cores, 2 * frames * z_part, len_y), jnp.bfloat16),
        [pltpu.SMEM] + [pltpu.VMEM] * 3,
        pltpu.VMEM,
        [pltpu.VMEM((steps, height, len_y), jnp.bfloat16)],
        4 * steps * height * len_y * len_y,
        4 * steps * height * len_y + 4 * len_y * len_y,
        VMEM_SOME,
    )(place, returned, own_maps, table)


def shards(image_estimate, coil_maps, measured, sampled_blocks, *tables):
    slabs = lax.axis_size("slab")
    groups = lax.axis_size("coil")
    _, frames, readout, z_lo, len_y = image_estimate.shape
    cores = 2
    z_part = z_lo // cores
    me = lax.axis_index("coil")
    place = jnp.stack([me // cores, me % cores]).astype(jnp.int32)

    outgoing = send_forward(coil_maps, image_estimate, tables[0], slabs)
    outgoing, coil_maps, measured, sampled_blocks = lax.optimization_barrier(
        (outgoing, coil_maps, measured, sampled_blocks)
    )
    arrived = lax.all_to_all(outgoing, "slab", split_axis=0, concat_axis=0, tiled=True)
    own_maps = maps_by_readout(coil_maps, place)
    upper = lax.axis_index("slab") >= slabs // 2
    measured = jnp.where(upper, lax.rev(measured, (4,)), measured)
    sampled_blocks = jnp.where(upper, lax.rev(sampled_blocks, (1,)), sampled_blocks)
    back_z = send_back(arrived, mirror(measured, 5), sampled_blocks, *tables[:2])
    returned = lax.all_to_all(
        back_z.reshape(slabs * groups, z_part, LANES),
        ("slab", "coil"),
        split_axis=0,
        concat_axis=0,
        tiled=True,
    )
    total = combine(
        returned.reshape(slabs, groups // cores, z_lo, LANES), own_maps, place, tables[2]
    )
    whole = lax.all_to_all(total, "coil", split_axis=0, concat_axis=0, tiled=True)
    whole = whole.reshape(readout, cores, 2, frames, z_part, len_y)
    whole = jnp.transpose(whole, (2, 3, 0, 1, 4, 5)).astype(jnp.float32)
    return whole.reshape(2, frames, readout, z_lo, len_y)


def solution(mesh):
    body = jax.shard_map(
        shards,
        mesh=mesh,
        in_specs=(
            P(None, None, None, "slab", None),
            P(None, "coil", None, "slab", None),
            P(None, None, None, "coil", "slab", None),
            P(None, "slab", None),
            *[P(None, None)] * 3,
        ),
        out_specs=P(None, None, None, "slab", None),
        check_vma=False,
    )

    def run(image_estimate, coil_maps, measured, sampled_blocks):
        slabs, len_y = mesh.shape["slab"], image_estimate.shape[4]
        tables = [jnp.asarray(table) for table in dft_tables(len_y, len_y // slabs)]
        return body(image_estimate, coil_maps, measured, sampled_blocks, *tables)

    return run
```

```python
import math

import jax
import jax.numpy as jnp
import ml_dtypes
import numpy as np
from jax import lax
from jax.experimental import pallas as pl
from jax.experimental.pallas import tpu as pltpu
from jax.sharding import PartitionSpec as P

LANES = 128
VMEM_SOME = 40 * 1024 * 1024
VMEM_ALL = 62 * 1024 * 1024


def dft_tables(length, run):
    indices = np.arange(length)
    angles = (indices[:, None] * indices[None, :] % length) * (2.0 * math.pi / length)
    cosine = (np.cos(angles) / math.sqrt(length)).astype(ml_dtypes.bfloat16)
    sine = (np.sin(angles) / math.sqrt(length)).astype(ml_dtypes.bfloat16)
    middle = length // 2
    turned = indices.reshape(-1, run).copy()
    turned[middle // run :] = turned[middle // run :, ::-1]
    turned = turned.reshape(-1)
    half_cos = cosine[:, :middle]
    half_sin = sine[:, :middle].copy()
    half_sin[:, 0] = cosine[:, middle]
    tables = (
        np.concatenate([half_cos, half_sin]),
        np.concatenate([half_cos.T, half_sin.T]),
        np.concatenate([cosine[turned], sine[turned]]),
    )
    return tuple(np.ascontiguousarray(table) for table in tables)


def mirror(values, axis):
    middle = values.shape[axis] // 2
    first = lax.slice_in_dim(values, 0, middle + 1, axis=axis)
    last = lax.slice_in_dim(values, middle + 1, 2 * middle, axis=axis)
    return lax.concatenate([first, lax.rev(last, (axis,))], axis)


def split_ends(by_cos, by_sin, axis):
    edge = (8, LANES)[axis]
    cos_edge = lax.slice_in_dim(by_cos, 0, edge, axis=axis)
    sin_edge = lax.slice_in_dim(by_sin, 0, edge, axis=axis)
    first = lax.broadcasted_iota(jnp.int32, cos_edge.shape, axis) == 0
    joined = []
    for edge_values, values in (
        (jnp.where(first, sin_edge, cos_edge), by_cos),
        (jnp.where(first, jnp.zeros_like(sin_edge), sin_edge), by_sin),
    ):
        rest = lax.slice_in_dim(values, edge, values.shape[axis], axis=axis)
        joined.append(jnp.concatenate([edge_values, rest], axis=axis))
    return joined


def swap_runs(blocks, run):
    count = len(blocks)
    rows, lanes = blocks[0].shape
    position = lax.broadcasted_iota(jnp.int32, (rows, lanes), 1) // run
    moved = [pltpu.roll(b, i * run, 1) if i else b for i, b in enumerate(blocks)]
    moved = [moved[-k % count] for k in range(count)]
    step = 1
    while step < count:
        chosen = (position & step) != 0
        moved = [jnp.where(chosen, moved[(k - step) % count], moved[k]) for k in range(count)]
        step *= 2
    return [pltpu.roll(b, lanes - j * run, 1) if j else b for j, b in enumerate(moved)]


def forward_y(
    maps_ref, image_ref, table_ref, out_ref, maps, image, table, lhs, out, arrive, leave
):
    _, coils, readout, z_lo, len_y = maps_ref.shape
    frames = image_ref.shape[1]
    steps = lhs.shape[0]
    part = readout // steps
    group = part * frames * coils
    half = group * z_lo
    run = LANES // group
    halves = [pl.ds(0, readout // 2), pl.ds(readout // 2, readout // 2)]
    inputs = [
        pltpu.make_async_copy(source.at[:, :, here], held.at[:, :, here], arrive.at[2 * k + n])
        for k, here in enumerate(halves)
        for n, (source, held) in enumerate(((maps_ref, maps), (image_ref, image)))
    ]
    fetch_table = pltpu.make_async_copy(table_ref, table, arrive.at[4])
    for copy in inputs + [fetch_table]:
        copy.start()
    for i in range(steps):
        if i * 2 % steps == 0:
            for copy in inputs[4 * i // steps : 4 * i // steps + 2]:
                copy.wait()
        for x in range(part):
            for f in range(frames):
                image_re = image[0, f, i * part + x].astype(jnp.float32)
                image_im = image[1, f, i * part + x].astype(jnp.float32)
                for c in range(coils):
                    map_re = maps[0, c, i * part + x].astype(jnp.float32)
                    map_im = maps[1, c, i * part + x].astype(jnp.float32)
                    row = ((x * frames + f) * coils + c) * z_lo
                    coil_re = map_re * image_re - map_im * image_im
                    coil_im = map_re * image_im + map_im * image_re
                    lhs[i, row : row + z_lo] = coil_re.astype(jnp.bfloat16)
                    lhs[i, row + half : row + half + z_lo] = coil_im.astype(jnp.bfloat16)
    fetch_table.wait()
    results = []
    for i in range(steps):
        by_cos = jnp.dot(lhs[i], table[:len_y], preferred_element_type=jnp.float32)
        by_sin = jnp.dot(lhs[i], table[len_y:], preferred_element_type=jnp.float32)
        middle = by_cos.shape[1]
        other_cos, by_sin = split_ends(by_cos, by_sin, 1)
        lower = (by_cos[:half] + by_sin[half:], by_cos[half:] - by_sin[:half])
        upper = (other_cos[:half] - by_sin[half:], other_cos[half:] + by_sin[:half])
        final = lax.broadcasted_iota(jnp.int32, (half, LANES), 1) == LANES - 1
        for p in range(2):
            lane = p * LANES
            blocks = [lower[p][:, t * LANES : (t + 1) * LANES] for t in range(middle // LANES)]
            moved = [
                pltpu.roll(upper[p][:, t * LANES : (t + 1) * LANES], LANES - 1, 1)
                for t in range(middle // LANES)
            ]
            for t in range(len(moved)):
                blocks.append(jnp.where(final, moved[(t + 1) % len(moved)], moved[t]))
            for t, block in enumerate(blocks):
                block = [block[u * z_lo : (u + 1) * z_lo] for u in range(group)]
                for u, rows in enumerate(swap_runs(block, run)):
                    slab = t * group + u
                    if t >= len(moved):
                        slab = out.shape[1] - 1 - (t - len(moved)) * group - u
                    out[i, slab, :, lane : lane + LANES] = rows.astype(jnp.bfloat16)
        lanes = pl.ds(2 * i * LANES, 2 * LANES)
        results.append(pltpu.make_async_copy(out.at[i], out_ref.at[:, :, lanes], leave.at[i]))
        results[-1].start()
    for copy in results:
        copy.wait()


def z_work(
    arrived_ref,
    measured_ref,
    weight_ref,
    columns_ref,
    rows_ref,
    out_ref,
    table,
    residual,
    out,
    leave,
):
    _, frames, readout, coils, ky_lo, len_z = measured_ref.shape
    width = weight_ref.shape[1]
    middle = len_z // 2
    steps = arrived_ref.shape[1] // (2 * width)
    part = readout // steps
    slabs, _, z_lo, _ = out_ref.shape
    for i in range(steps):
        start, mid, end = 2 * i * width, (2 * i + 1) * width, (2 * i + 2) * width
        arrived = arrived_ref[:, start:end]
        by_cos = jnp.dot(rows_ref[:middle], arrived, preferred_element_type=jnp.float32)
        by_sin = jnp.dot(rows_ref[middle:], arrived, preferred_element_type=jnp.float32)
        other_cos, by_sin = split_ends(by_cos, by_sin, 0)
        target = []
        for p in range(2):
            lines = [
                measured_ref[p, f, i * part + x].reshape(coils * ky_lo, len_z)
                for x in range(part)
                for f in range(frames)
            ]
            target.append(jnp.concatenate(lines, axis=0).T.astype(jnp.float32))
        for rows, spectrum_re, spectrum_im in (
            (
                slice(0, middle),
                by_cos[:, :width] + by_sin[:, width:],
                by_cos[:, width:] - by_sin[:, :width],
            ),
            (
                slice(middle, len_z),
                other_cos[:, :width] - by_sin[:, width:],
                other_cos[:, width:] + by_sin[:, :width],
            ),
        ):
            weight = weight_ref[rows]
            residual[rows, start:mid] = (weight * (spectrum_re - target[0][rows])).astype(jnp.bfloat16)
            residual[rows, mid:end] = (weight * (spectrum_im - target[1][rows])).astype(jnp.bfloat16)
    run = width // part
    lower = lax.broadcasted_iota(jnp.int32, (len_z, width), 1) < run
    half_cos, half_sin = columns_ref[:len_z], columns_ref[len_z:]
    other_cos, half_sin = split_ends(half_cos, half_sin, 1)
    table[:len_z, :middle] = half_cos
    table[:len_z, middle:] = other_cos
    table[len_z:, :middle] = half_sin
    table[len_z:, middle:] = -half_sin
    copies = []
    for i in range(steps):
        rows = residual[:, 2 * i * width : (2 * i + 2) * width]
        by_cos = jnp.dot(table[:len_z], rows, preferred_element_type=jnp.float32)
        by_sin = jnp.dot(table[len_z:], rows, preferred_element_type=jnp.float32)
        back_re = by_cos[:, :width] - by_sin[:, width:]
        back_im = by_cos[:, width:] + by_sin[:, :width]
        sent = (
            jnp.where(lower, back_re, pltpu.roll(back_im, run, 1)),
            jnp.where(lower, pltpu.roll(back_re, run, 1), back_im),
        )
        for x in range(part):
            out[:, i * part + x] = sent[x].reshape(slabs, z_lo, width).astype(jnp.bfloat16)
        here = pl.ds(i * part, part)
        copies.append(pltpu.make_async_copy(out.at[:, here], out_ref.at[:, here], leave.at[i]))
        copies[-1].start()
    for copy in copies:
        copy.wait()


def backward_y(place_ref, returned_ref, maps_ref, table_ref, out_ref, lhs):
    chip, core = place_ref[0], place_ref[1]
    _, chips, rows, _ = returned_ref.shape
    _, cores, _, coils, z_part, len_y = maps_ref.shape
    steps, height, _ = lhs.shape
    pair = chips // steps
    half = height // 2
    frames = half // (pair * coils * rows)
    group = 2 * frames * coils
    run = LANES // group
    zero = jnp.zeros((z_part, len_y), jnp.float32)
    sums = [[zero, zero] for _ in range(frames)]
    for i in range(steps):
        for q in range(pair):
            for t in range(len_y // LANES):
                block = returned_ref[t * group : (t + 1) * group, i * pair + q].astype(jnp.float32)
                block = swap_runs([block[u] for u in range(group)], run)
                for p in range(2):
                    for f in range(frames):
                        for c in range(coils):
                            row = p * half + ((f * pair + q) * coils + c) * rows
                            lhs[i, row : row + rows, t * LANES : (t + 1) * LANES] = block[
                                (p * frames + f) * coils + c
                            ].astype(jnp.bfloat16)
        by_cos = jnp.dot(lhs[i], table_ref[:len_y], preferred_element_type=jnp.float32)
        by_sin = jnp.dot(lhs[i], table_ref[len_y:], preferred_element_type=jnp.float32)
        back_re = by_cos[:half] - by_sin[half:]
        back_im = by_cos[half:] + by_sin[:half]
        for q in range(pair):
            source = (i * pair + q) ^ chip
            for k in range(cores):
                for c in range(coils):
                    map_re = maps_ref[source, k ^ core, 0, c].astype(jnp.float32)
                    map_im = maps_ref[source, k ^ core, 1, c].astype(jnp.float32)
                    for f in range(frames):
                        row = ((f * pair + q) * coils + c) * rows + k * z_part
                        re, im = back_re[row : row + z_part], back_im[row : row + z_part]
                        sums[f][0] = sums[f][0] + (map_re * re + map_im * im)
                        sums[f][1] = sums[f][1] + (map_re * im - map_im * re)
    whole = jnp.concatenate([sums[f][p] for p in range(2) for f in range(frames)], axis=0)
    out_ref[...] = jnp.broadcast_to(whole.astype(jnp.bfloat16)[None], out_ref.shape)


def call(kernel, name, out_shape, in_spaces, out_space, scratch, flops, bytes_accessed, vmem):
    return pl.pallas_call(
        kernel,
        name=name,
        out_shape=out_shape,
        in_specs=[pl.BlockSpec(memory_space=space) for space in in_spaces],
        out_specs=pl.BlockSpec(memory_space=out_space),
        scratch_shapes=scratch,
        compiler_params=pltpu.CompilerParams(vmem_limit_bytes=vmem),
        cost_estimate=pl.CostEstimate(
            flops=flops, bytes_accessed=bytes_accessed, transcendentals=0
        ),
    )


def maps_by_readout(coil_maps, place):
    cores = 2
    chips = lax.axis_size("coil") // cores
    chip, core = place[0], place[1]
    _, coils, readout, z_lo, len_y = coil_maps.shape
    halves = coil_maps.reshape(2, coils, readout, cores, z_lo // cores, len_y)
    own = lax.dynamic_index_in_dim(halves, core, 3, keepdims=False)
    other = lax.dynamic_index_in_dim(halves, 1 - core, 3, keepdims=False)
    devices = range(chips * cores)
    got = lax.ppermute(other, "coil", [(i, i ^ 1) for i in devices])
    both = jnp.stack([own, got])
    pieces = []
    for k in range(chips):
        piece = lax.dynamic_index_in_dim(both, chip ^ k, 3, keepdims=False)
        if k:
            piece = lax.ppermute(piece, "coil", [(i, i ^ (cores * k)) for i in devices])
        pieces.append(piece)
    return jnp.stack(pieces)


def send_forward(coil_maps, image_estimate, table, slabs):
    _, frames, readout, z_lo, len_y = image_estimate.shape
    coils = coil_maps.shape[1]
    group = LANES // (len_y // slabs)
    part = group // (coils * frames)
    steps = readout // part
    half = group * z_lo
    return call(
        forward_y,
        "forward_y",
        jax.ShapeDtypeStruct((slabs, z_lo, steps * 2 * LANES), jnp.bfloat16),
        [pl.ANY] * 3,
        pl.ANY,
        [
            pltpu.VMEM(coil_maps.shape, jnp.bfloat16),
            pltpu.VMEM(image_estimate.shape, jnp.bfloat16),
            pltpu.VMEM(table.shape, jnp.bfloat16),
            pltpu.VMEM((steps, 2 * half, len_y), jnp.bfloat16),
            pltpu.VMEM((steps, slabs, z_lo, 2 * LANES), jnp.bfloat16),
            pltpu.SemaphoreType.DMA((5,)),
            pltpu.SemaphoreType.DMA((steps,)),
        ],
        4 * steps * half * len_y * len_y,
        8 * steps * half * len_y + 2 * len_y * len_y,
        VMEM_ALL,
    )(coil_maps, image_estimate, table)


def send_back(arrived, measured, sampled_blocks, columns, rows):
    slabs, z_lo, lanes = arrived.shape
    _, frames, readout, coils, ky_lo, len_z = measured.shape
    block_count = sampled_blocks.shape[2]
    steps = lanes // (2 * LANES)
    part = readout // steps
    weight = jnp.transpose(sampled_blocks.astype(jnp.float32), (2, 0, 1))[:, None, :, None, :]
    weight = jnp.broadcast_to(weight, (block_count, part, frames, coils, ky_lo))
    weight = jnp.repeat(weight.reshape(block_count, LANES), len_z // block_count, axis=0)
    return call(
        z_work,
        "z_work",
        jax.ShapeDtypeStruct((slabs, readout, z_lo, LANES), jnp.bfloat16),
        [pltpu.VMEM] * 5,
        pl.ANY,
        [
            pltpu.VMEM((2 * len_z, len_z), jnp.bfloat16),
            pltpu.VMEM((len_z, lanes), jnp.bfloat16),
            pltpu.VMEM((slabs, readout, z_lo, LANES), jnp.bfloat16),
            pltpu.SemaphoreType.DMA((steps,)),
        ],
        6 * lanes * len_z * len_z,
        6 * lanes * len_z + 4 * len_z * len_z,
        VMEM_SOME,
    )(arrived.reshape(len_z, lanes), measured, mirror(weight, 0), columns, rows)


def combine(returned, own_maps, place, table):
    slabs, chips, z_lo, _ = returned.shape
    _, cores, _, coils, z_part, len_y = own_maps.shape
    frames = LANES // (len_y // slabs * 2 * coils)
    pair = 2
    steps = chips // pair
    height = 2 * frames * pair * coils * z_lo
    return call(
        backward_y,
        "backward_y",
        jax.ShapeDtypeStruct((chips * cores, 2 * frames * z_part, len_y), jnp.bfloat16),
        [pltpu.SMEM] + [pltpu.VMEM] * 3,
        pltpu.VMEM,
        [pltpu.VMEM((steps, height, len_y), jnp.bfloat16)],
        4 * steps * height * len_y * len_y,
        4 * steps * height * len_y + 4 * len_y * len_y,
        VMEM_SOME,
    )(place, returned, own_maps, table)


def shards(image_estimate, coil_maps, measured, sampled_blocks, *tables):
    slabs = lax.axis_size("slab")
    groups = lax.axis_size("coil")
    _, frames, readout, z_lo, len_y = image_estimate.shape
    cores = 2
    z_part = z_lo // cores
    me = lax.axis_index("coil")
    place = jnp.stack([me // cores, me % cores]).astype(jnp.int32)

    outgoing = send_forward(coil_maps, image_estimate, tables[0], slabs)
    outgoing, coil_maps, measured, sampled_blocks = lax.optimization_barrier(
        (outgoing, coil_maps, measured, sampled_blocks)
    )
    arrived = lax.all_to_all(outgoing, "slab", split_axis=0, concat_axis=0, tiled=True)
    own_maps = maps_by_readout(coil_maps, place)
    upper = lax.axis_index("slab") >= slabs // 2
    measured = jnp.where(upper, lax.rev(measured, (4,)), measured)
    sampled_blocks = jnp.where(upper, lax.rev(sampled_blocks, (1,)), sampled_blocks)
    back_z = send_back(arrived, mirror(measured, 5), sampled_blocks, *tables[:2])
    returned = lax.all_to_all(
        back_z.reshape(slabs * groups, z_part, LANES),
        ("slab", "coil"),
        split_axis=0,
        concat_axis=0,
        tiled=True,
    )
    total = combine(
        returned.reshape(slabs, groups // cores, z_lo, LANES), own_maps, place, tables[2]
    )
    whole = lax.all_to_all(total, "coil", split_axis=0, concat_axis=0, tiled=True)
    whole = whole.reshape(readout, cores, 2, frames, z_part, len_y)
    whole = jnp.transpose(whole, (2, 3, 0, 1, 4, 5)).astype(jnp.float32)
    return whole.reshape(2, frames, readout, z_lo, len_y)


def solution(mesh):
    body = jax.shard_map(
        shards,
        mesh=mesh,
        in_specs=(
            P(None, None, None, "slab", None),
            P(None, "coil", None, "slab", None),
            P(None, None, None, "coil", "slab", None),
            P(None, "slab", None),
            *[P(None, None)] * 3,
        ),
        out_specs=P(None, None, None, "slab", None),
        check_vma=False,
    )

    def run(image_estimate, coil_maps, measured, sampled_blocks):
        slabs, len_y = mesh.shape["slab"], image_estimate.shape[4]
        tables = [jnp.asarray(table) for table in dft_tables(len_y, len_y // slabs)]
        return body(image_estimate, coil_maps, measured, sampled_blocks, *tables)

    return run
```

```python
import math

import jax
import jax.numpy as jnp
import ml_dtypes
import numpy as np
from jax import lax
from jax.experimental import pallas as pl
from jax.experimental.pallas import tpu as pltpu
from jax.sharding import PartitionSpec as P

LANES = 128
VMEM_SOME = 40 * 1024 * 1024
VMEM_ALL = 62 * 1024 * 1024


def dft_tables(length, run):
    indices = np.arange(length)
    angles = (indices[:, None] * indices[None, :] % length) * (2.0 * math.pi / length)
    cosine = (np.cos(angles) / math.sqrt(length)).astype(ml_dtypes.bfloat16)
    sine = (np.sin(angles) / math.sqrt(length)).astype(ml_dtypes.bfloat16)
    middle = length // 2
    turned = indices.reshape(-1, run).copy()
    turned[middle // run :] = turned[middle // run :, ::-1]
    turned = turned.reshape(-1)
    half_cos = cosine[:, :middle]
    half_sin = sine[:, :middle].copy()
    half_sin[:, 0] = cosine[:, middle]
    tables = (
        np.concatenate([half_cos, half_sin]),
        np.concatenate([half_cos.T, half_sin.T]),
        np.concatenate([cosine[turned], sine[turned]]),
    )
    return tuple(np.ascontiguousarray(table) for table in tables)


def mirror(values, axis):
    middle = values.shape[axis] // 2
    first = lax.slice_in_dim(values, 0, middle + 1, axis=axis)
    last = lax.slice_in_dim(values, middle + 1, 2 * middle, axis=axis)
    return lax.concatenate([first, lax.rev(last, (axis,))], axis)


def split_ends(by_cos, by_sin, axis):
    edge = (8, LANES)[axis]
    cos_edge = lax.slice_in_dim(by_cos, 0, edge, axis=axis)
    sin_edge = lax.slice_in_dim(by_sin, 0, edge, axis=axis)
    first = lax.broadcasted_iota(jnp.int32, cos_edge.shape, axis) == 0
    joined = []
    for edge_values, values in (
        (jnp.where(first, sin_edge, cos_edge), by_cos),
        (jnp.where(first, jnp.zeros_like(sin_edge), sin_edge), by_sin),
    ):
        rest = lax.slice_in_dim(values, edge, values.shape[axis], axis=axis)
        joined.append(jnp.concatenate([edge_values, rest], axis=axis))
    return joined


def swap_runs(blocks, run):
    count = len(blocks)
    rows, lanes = blocks[0].shape
    position = lax.broadcasted_iota(jnp.int32, (rows, lanes), 1) // run
    moved = [pltpu.roll(b, i * run, 1) if i else b for i, b in enumerate(blocks)]
    moved = [moved[-k % count] for k in range(count)]
    step = 1
    while step < count:
        chosen = (position & step) != 0
        moved = [jnp.where(chosen, moved[(k - step) % count], moved[k]) for k in range(count)]
        step *= 2
    return [pltpu.roll(b, lanes - j * run, 1) if j else b for j, b in enumerate(moved)]


def forward_y(
    maps_ref, image_ref, table_ref, out_ref, maps, image, table, lhs, out, arrive, leave
):
    _, coils, readout, z_lo, len_y = maps_ref.shape
    frames = image_ref.shape[1]
    steps = lhs.shape[0]
    part = readout // steps
    group = part * frames * coils
    half = group * z_lo
    run = LANES // group
    halves = [pl.ds(0, readout // 2), pl.ds(readout // 2, readout // 2)]
    inputs = [
        pltpu.make_async_copy(source.at[:, :, here], held.at[:, :, here], arrive.at[2 * k + n])
        for k, here in enumerate(halves)
        for n, (source, held) in enumerate(((maps_ref, maps), (image_ref, image)))
    ]
    fetch_table = [
        pltpu.make_async_copy(table_ref.at[rows], table.at[rows], arrive.at[4 + k])
        for k, rows in enumerate((pl.ds(0, len_y), pl.ds(len_y, len_y)))
    ]
    for copy in inputs + fetch_table:
        copy.start()
    for i in range(steps):
        if i * 2 % steps == 0:
            for copy in inputs[4 * i // steps : 4 * i // steps + 2]:
                copy.wait()
        for x in range(part):
            for f in range(frames):
                image_re = image[0, f, i * part + x].astype(jnp.float32)
                image_im = image[1, f, i * part + x].astype(jnp.float32)
                for c in range(coils):
                    map_re = maps[0, c, i * part + x].astype(jnp.float32)
                    map_im = maps[1, c, i * part + x].astype(jnp.float32)
                    row = ((x * frames + f) * coils + c) * z_lo
                    coil_re = map_re * image_re - map_im * image_im
                    coil_im = map_re * image_im + map_im * image_re
                    lhs[i, row : row + z_lo] = coil_re.astype(jnp.bfloat16)
                    lhs[i, row + half : row + half + z_lo] = coil_im.astype(jnp.bfloat16)
    fetch_table[0].wait()
    results = []
    for i in range(steps):
        by_cos = jnp.dot(lhs[i], table[:len_y], preferred_element_type=jnp.float32)
        if i == 0:
            fetch_table[1].wait()
        by_sin = jnp.dot(lhs[i], table[len_y:], preferred_element_type=jnp.float32)
        middle = by_cos.shape[1]
        other_cos, by_sin = split_ends(by_cos, by_sin, 1)
        lower = (by_cos[:half] + by_sin[half:], by_cos[half:] - by_sin[:half])
        upper = (other_cos[:half] - by_sin[half:], other_cos[half:] + by_sin[:half])
        final = lax.broadcasted_iota(jnp.int32, (half, LANES), 1) == LANES - 1
        for p in range(2):
            lane = p * LANES
            blocks = [lower[p][:, t * LANES : (t + 1) * LANES] for t in range(middle // LANES)]
            moved = [
                pltpu.roll(upper[p][:, t * LANES : (t + 1) * LANES], LANES - 1, 1)
                for t in range(middle // LANES)
            ]
            for t in range(len(moved)):
                blocks.append(jnp.where(final, moved[(t + 1) % len(moved)], moved[t]))
            for t, block in enumerate(blocks):
                block = [block[u * z_lo : (u + 1) * z_lo] for u in range(group)]
                for u, rows in enumerate(swap_runs(block, run)):
                    slab = t * group + u
                    if t >= len(moved):
                        slab = out.shape[1] - 1 - (t - len(moved)) * group - u
                    out[i, slab, :, lane : lane + LANES] = rows.astype(jnp.bfloat16)
        lanes = pl.ds(2 * i * LANES, 2 * LANES)
        results.append(pltpu.make_async_copy(out.at[i], out_ref.at[:, :, lanes], leave.at[i]))
        results[-1].start()
    for copy in results:
        copy.wait()


def z_work(
    arrived_ref,
    measured_ref,
    weight_ref,
    columns_ref,
    rows_ref,
    out_ref,
    table,
    residual,
    out,
    leave,
):
    _, frames, readout, coils, ky_lo, len_z = measured_ref.shape
    width = weight_ref.shape[1]
    middle = len_z // 2
    steps = arrived_ref.shape[1] // (2 * width)
    part = readout // steps
    slabs, _, z_lo, _ = out_ref.shape
    for i in range(steps):
        start, mid, end = 2 * i * width, (2 * i + 1) * width, (2 * i + 2) * width
        arrived = arrived_ref[:, start:end]
        by_cos = jnp.dot(rows_ref[:middle], arrived, preferred_element_type=jnp.float32)
        by_sin = jnp.dot(rows_ref[middle:], arrived, preferred_element_type=jnp.float32)
        other_cos, by_sin = split_ends(by_cos, by_sin, 0)
        target = []
        for p in range(2):
            lines = [
                measured_ref[p, f, i * part + x].reshape(coils * ky_lo, len_z)
                for x in range(part)
                for f in range(frames)
            ]
            target.append(jnp.concatenate(lines, axis=0).T.astype(jnp.float32))
        for rows, spectrum_re, spectrum_im in (
            (
                slice(0, middle),
                by_cos[:, :width] + by_sin[:, width:],
                by_cos[:, width:] - by_sin[:, :width],
            ),
            (
                slice(middle, len_z),
                other_cos[:, :width] - by_sin[:, width:],
                other_cos[:, width:] + by_sin[:, :width],
            ),
        ):
            weight = weight_ref[rows]
            residual[rows, start:mid] = (weight * (spectrum_re - target[0][rows])).astype(jnp.bfloat16)
            residual[rows, mid:end] = (weight * (spectrum_im - target[1][rows])).astype(jnp.bfloat16)
    run = width // part
    lower = lax.broadcasted_iota(jnp.int32, (len_z, width), 1) < run
    half_cos, half_sin = columns_ref[:len_z], columns_ref[len_z:]
    other_cos, half_sin = split_ends(half_cos, half_sin, 1)
    table[:len_z, :middle] = half_cos
    table[:len_z, middle:] = other_cos
    table[len_z:, :middle] = half_sin
    table[len_z:, middle:] = -half_sin
    copies = []
    for i in range(steps):
        rows = residual[:, 2 * i * width : (2 * i + 2) * width]
        by_cos = jnp.dot(table[:len_z], rows, preferred_element_type=jnp.float32)
        by_sin = jnp.dot(table[len_z:], rows, preferred_element_type=jnp.float32)
        back_re = by_cos[:, :width] - by_sin[:, width:]
        back_im = by_cos[:, width:] + by_sin[:, :width]
        sent = (
            jnp.where(lower, back_re, pltpu.roll(back_im, run, 1)),
            jnp.where(lower, pltpu.roll(back_re, run, 1), back_im),
        )
        for x in range(part):
            out[:, i * part + x] = sent[x].reshape(slabs, z_lo, width).astype(jnp.bfloat16)
        here = pl.ds(i * part, part)
        copies.append(pltpu.make_async_copy(out.at[:, here], out_ref.at[:, here], leave.at[i]))
        copies[-1].start()
    for copy in copies:
        copy.wait()


def backward_y(place_ref, returned_ref, maps_ref, table_ref, out_ref, lhs):
    chip, core = place_ref[0], place_ref[1]
    _, chips, rows, _ = returned_ref.shape
    _, cores, _, coils, z_part, len_y = maps_ref.shape
    steps, height, _ = lhs.shape
    pair = chips // steps
    half = height // 2
    frames = half // (pair * coils * rows)
    group = 2 * frames * coils
    run = LANES // group
    zero = jnp.zeros((z_part, len_y), jnp.float32)
    sums = [[zero, zero] for _ in range(frames)]
    for i in range(steps):
        for q in range(pair):
            for t in range(len_y // LANES):
                block = returned_ref[t * group : (t + 1) * group, i * pair + q].astype(jnp.float32)
                block = swap_runs([block[u] for u in range(group)], run)
                for p in range(2):
                    for f in range(frames):
                        for c in range(coils):
                            row = p * half + ((f * pair + q) * coils + c) * rows
                            lhs[i, row : row + rows, t * LANES : (t + 1) * LANES] = block[
                                (p * frames + f) * coils + c
                            ].astype(jnp.bfloat16)
        by_cos = jnp.dot(lhs[i], table_ref[:len_y], preferred_element_type=jnp.float32)
        by_sin = jnp.dot(lhs[i], table_ref[len_y:], preferred_element_type=jnp.float32)
        back_re = by_cos[:half] - by_sin[half:]
        back_im = by_cos[half:] + by_sin[:half]
        for q in range(pair):
            source = (i * pair + q) ^ chip
            for k in range(cores):
                for c in range(coils):
                    map_re = maps_ref[source, k ^ core, 0, c].astype(jnp.float32)
                    map_im = maps_ref[source, k ^ core, 1, c].astype(jnp.float32)
                    for f in range(frames):
                        row = ((f * pair + q) * coils + c) * rows + k * z_part
                        re, im = back_re[row : row + z_part], back_im[row : row + z_part]
                        sums[f][0] = sums[f][0] + (map_re * re + map_im * im)
                        sums[f][1] = sums[f][1] + (map_re * im - map_im * re)
    whole = jnp.concatenate([sums[f][p] for p in range(2) for f in range(frames)], axis=0)
    out_ref[...] = jnp.broadcast_to(whole.astype(jnp.bfloat16)[None], out_ref.shape)


def call(kernel, name, out_shape, in_spaces, out_space, scratch, flops, bytes_accessed, vmem):
    return pl.pallas_call(
        kernel,
        name=name,
        out_shape=out_shape,
        in_specs=[pl.BlockSpec(memory_space=space) for space in in_spaces],
        out_specs=pl.BlockSpec(memory_space=out_space),
        scratch_shapes=scratch,
        compiler_params=pltpu.CompilerParams(vmem_limit_bytes=vmem),
        cost_estimate=pl.CostEstimate(
            flops=flops, bytes_accessed=bytes_accessed, transcendentals=0
        ),
    )


def maps_by_readout(coil_maps, place):
    cores = 2
    chips = lax.axis_size("coil") // cores
    chip, core = place[0], place[1]
    _, coils, readout, z_lo, len_y = coil_maps.shape
    halves = coil_maps.reshape(2, coils, readout, cores, z_lo // cores, len_y)
    own = lax.dynamic_index_in_dim(halves, core, 3, keepdims=False)
    other = lax.dynamic_index_in_dim(halves, 1 - core, 3, keepdims=False)
    devices = range(chips * cores)
    got = lax.ppermute(other, "coil", [(i, i ^ 1) for i in devices])
    both = jnp.stack([own, got])
    pieces = []
    for k in range(chips):
        piece = lax.dynamic_index_in_dim(both, chip ^ k, 3, keepdims=False)
        if k:
            piece = lax.ppermute(piece, "coil", [(i, i ^ (cores * k)) for i in devices])
        pieces.append(piece)
    return jnp.stack(pieces)


def send_forward(coil_maps, image_estimate, table, slabs):
    _, frames, readout, z_lo, len_y = image_estimate.shape
    coils = coil_maps.shape[1]
    group = LANES // (len_y // slabs)
    part = group // (coils * frames)
    steps = readout // part
    half = group * z_lo
    return call(
        forward_y,
        "forward_y",
        jax.ShapeDtypeStruct((slabs, z_lo, steps * 2 * LANES), jnp.bfloat16),
        [pl.ANY] * 3,
        pl.ANY,
        [
            pltpu.VMEM(coil_maps.shape, jnp.bfloat16),
            pltpu.VMEM(image_estimate.shape, jnp.bfloat16),
            pltpu.VMEM(table.shape, jnp.bfloat16),
            pltpu.VMEM((steps, 2 * half, len_y), jnp.bfloat16),
            pltpu.VMEM((steps, slabs, z_lo, 2 * LANES), jnp.bfloat16),
            pltpu.SemaphoreType.DMA((6,)),
            pltpu.SemaphoreType.DMA((steps,)),
        ],
        4 * steps * half * len_y * len_y,
        8 * steps * half * len_y + 2 * len_y * len_y,
        VMEM_ALL,
    )(coil_maps, image_estimate, table)


def send_back(arrived, measured, sampled_blocks, columns, rows):
    slabs, z_lo, lanes = arrived.shape
    _, frames, readout, coils, ky_lo, len_z = measured.shape
    block_count = sampled_blocks.shape[2]
    steps = lanes // (2 * LANES)
    part = readout // steps
    weight = jnp.transpose(sampled_blocks.astype(jnp.float32), (2, 0, 1))[:, None, :, None, :]
    weight = jnp.broadcast_to(weight, (block_count, part, frames, coils, ky_lo))
    weight = jnp.repeat(weight.reshape(block_count, LANES), len_z // block_count, axis=0)
    return call(
        z_work,
        "z_work",
        jax.ShapeDtypeStruct((slabs, readout, z_lo, LANES), jnp.bfloat16),
        [pltpu.VMEM] * 5,
        pl.ANY,
        [
            pltpu.VMEM((2 * len_z, len_z), jnp.bfloat16),
            pltpu.VMEM((len_z, lanes), jnp.bfloat16),
            pltpu.VMEM((slabs, readout, z_lo, LANES), jnp.bfloat16),
            pltpu.SemaphoreType.DMA((steps,)),
        ],
        6 * lanes * len_z * len_z,
        6 * lanes * len_z + 4 * len_z * len_z,
        VMEM_SOME,
    )(arrived.reshape(len_z, lanes), measured, mirror(weight, 0), columns, rows)


def combine(returned, own_maps, place, table):
    slabs, chips, z_lo, _ = returned.shape
    _, cores, _, coils, z_part, len_y = own_maps.shape
    frames = LANES // (len_y // slabs * 2 * coils)
    pair = 2
    steps = chips // pair
    height = 2 * frames * pair * coils * z_lo
    return call(
        backward_y,
        "backward_y",
        jax.ShapeDtypeStruct((chips * cores, 2 * frames * z_part, len_y), jnp.bfloat16),
        [pltpu.SMEM] + [pltpu.VMEM] * 3,
        pltpu.VMEM,
        [pltpu.VMEM((steps, height, len_y), jnp.bfloat16)],
        4 * steps * height * len_y * len_y,
        4 * steps * height * len_y + 4 * len_y * len_y,
        VMEM_SOME,
    )(place, returned, own_maps, table)


def shards(image_estimate, coil_maps, measured, sampled_blocks, *tables):
    slabs = lax.axis_size("slab")
    groups = lax.axis_size("coil")
    _, frames, readout, z_lo, len_y = image_estimate.shape
    cores = 2
    z_part = z_lo // cores
    me = lax.axis_index("coil")
    place = jnp.stack([me // cores, me % cores]).astype(jnp.int32)

    outgoing = send_forward(coil_maps, image_estimate, tables[0], slabs)
    outgoing, coil_maps, measured, sampled_blocks = lax.optimization_barrier(
        (outgoing, coil_maps, measured, sampled_blocks)
    )
    arrived = lax.all_to_all(outgoing, "slab", split_axis=0, concat_axis=0, tiled=True)
    own_maps = maps_by_readout(coil_maps, place)
    upper = lax.axis_index("slab") >= slabs // 2
    measured = jnp.where(upper, lax.rev(measured, (4,)), measured)
    sampled_blocks = jnp.where(upper, lax.rev(sampled_blocks, (1,)), sampled_blocks)
    back_z = send_back(arrived, mirror(measured, 5), sampled_blocks, *tables[:2])
    returned = lax.all_to_all(
        back_z.reshape(slabs * groups, z_part, LANES),
        ("slab", "coil"),
        split_axis=0,
        concat_axis=0,
        tiled=True,
    )
    total = combine(
        returned.reshape(slabs, groups // cores, z_lo, LANES), own_maps, place, tables[2]
    )
    whole = lax.all_to_all(total, "coil", split_axis=0, concat_axis=0, tiled=True)
    whole = whole.reshape(readout, cores, 2, frames, z_part, len_y)
    whole = jnp.transpose(whole, (2, 3, 0, 1, 4, 5)).astype(jnp.float32)
    return whole.reshape(2, frames, readout, z_lo, len_y)


def solution(mesh):
    body = jax.shard_map(
        shards,
        mesh=mesh,
        in_specs=(
            P(None, None, None, "slab", None),
            P(None, "coil", None, "slab", None),
            P(None, None, None, "coil", "slab", None),
            P(None, "slab", None),
            *[P(None, None)] * 3,
        ),
        out_specs=P(None, None, None, "slab", None),
        check_vma=False,
    )

    def run(image_estimate, coil_maps, measured, sampled_blocks):
        slabs, len_y = mesh.shape["slab"], image_estimate.shape[4]
        tables = [jnp.asarray(table) for table in dft_tables(len_y, len_y // slabs)]
        return body(image_estimate, coil_maps, measured, sampled_blocks, *tables)

    return run
```
